32 devices in a mesh: corpus: 2 (over x), rows: 8 (over z, y), feat: 2 (over core).
Axes of the slice: x: 2, y: 2, z: 4, core: 2. Of those that a mesh axis runs over, the one named last changes fastest.
Arguments:
- queries: bfloat16 [1024, 4096], P('rows', 'feat'), may hold values from -6 to 6
- kernel: bfloat16 [8192, 4096], P(('corpus', 'feat'), 'rows'), parts along dimension 0, may hold values from -0.09375 to 0.09375
- train_feats: bfloat16 [65536, 4096], P(('corpus', 'rows', 'feat')), parts along dimension 0, may hold values from -6 to 6
Outputs:
- scores: bfloat16 [1024, 65536], P(('rows', 'feat'), 'corpus'), parts along dimension 1
The draws below stay inside these ranges and needn't reach their ends.
There are 2 independent parts, one for each index of `corpus`. The reference program is written for one: setup_inputs(seed, part) draws one part's arguments, and reference() takes and returns one part's arrays. A program takes and returns all parts, laid end to end along the dimension named above; an argument that names none is the same for every part. Nothing has to cross between parts.
All inputs are finite; a program needn't handle non-finite values.
Results may differ from the reference program's by a relative error of at most 0.005.
Values may be sent and summed in bfloat16 or wider, within the bound.
No kernel may reach another device: no remote copies, remote signals or barrier semaphores. Data moves between devices by JAX's collectives and lax.ppermute only.
A program may use at most 128 MiB of HBM per device.

```python
import jax
import jax.numpy as jnp
from jax import lax

P_SIZE = 4096
NQ = 1024
NTRAIN = 32768


def block_scale(own_key, shape, split, low, high):
    level = 1.0
    for axis_at, blocks in split:
        steps = jax.random.uniform(jax.random.fold_in(jax.random.fold_in(own_key, 6), axis_at), (blocks,), jnp.float32, low / len(split), high / len(split))
        level = level * jnp.repeat(jnp.exp(steps), shape[axis_at] // blocks).reshape((-1,) + (1,) * (len(shape) - 1 - axis_at))
    return level


def bell_draw(rng, dims, spread, limit, cuts=(), dtype=jnp.bfloat16):
    result = jax.random.normal(rng, dims, jnp.float32) * spread
    if len(cuts) > 0:
        result = block_scale(rng, dims, cuts, -0.22, 0.18) * result
    return jnp.clip(result, min=-limit, max=limit).astype(dtype)


def setup_inputs(seed: int = 0, part: int = 0) -> dict:
    streams_of = jax.random.split(jax.random.key(seed), 4)
    part_keys = jax.random.split(jax.random.fold_in(streams_of[3], part), 4)
    return {
        "queries": bell_draw(streams_of[0], (NQ, P_SIZE), 1.0, 6.0, ((0, 8), (1, 2))),
        "kernel": bell_draw(part_keys[1], (P_SIZE, P_SIZE), P_SIZE ** -0.5, 0.09375, ((0, 2), (1, 8))),
        "train_feats": bell_draw(part_keys[2], (NTRAIN, P_SIZE), 1.0, 6.0, ((0, 16),)),
    }


epsilon = 1e-06

def reference(queries, kernel, train_feats):
    precond = jnp.dot(queries, kernel, preferred_element_type=jnp.float32).astype(jnp.bfloat16)
    widened = precond.astype(jnp.float32)
    lengths = jnp.sqrt(lax.optimization_barrier(jnp.sum(widened * widened, axis=1)) + epsilon)
    raw = jnp.dot(precond, train_feats.T, preferred_element_type=jnp.float32)
    return (raw / lengths[:, None]).astype(jnp.bfloat16)
```

```python
import functools

import jax
import jax.numpy as jnp
from jax import lax
from jax.sharding import PartitionSpec as P

epsilon = 1e-06


def ring_order(n):
    if n == 8:
        return [0, 2, 4, 6, 7, 5, 3, 1]
    return list(range(n))


def walk(block, n, order):
    ahead = [(order[i], order[(i + 1) % n]) for i in range(n)]
    back = [(b, a) for a, b in ahead]
    place = jnp.array([order.index(i) for i in range(n)])[lax.axis_index("rows")]
    ring = jnp.array(order)
    yield [(ring[place], 0, block)]
    forward = backward = block
    for step in range(1, n // 2):
        forward = lax.ppermute(forward, "rows", ahead)
        backward = lax.ppermute(backward, "rows", back)
        yield [(ring[(place - step) % n], 0, forward), (ring[(place + step) % n], 0, backward)]
    half = block.shape[0] // 2
    owner = ring[(place + n // 2) % n]
    top = lax.ppermute(forward[:half], "rows", ahead)
    bottom = lax.ppermute(backward[half:], "rows", back)
    yield [(owner, 0, top), (owner, half, bottom)]


def per_device(n, queries, kernel, train_feats):
    order = ring_order(n)
    feat = lax.axis_index("feat")
    me = lax.axis_index("rows") * 2 + feat
    swap = [(0, 1), (1, 0)]
    count = queries.shape[0]
    width = kernel.shape[1]
    half = width // 2
    total = count * n

    mine = jnp.zeros((total, half), jnp.bfloat16)
    for arrived in walk(queries, n, order):
        for owner, first, block in arrived:
            partial = jnp.dot(block, kernel, preferred_element_type=jnp.float32)
            keep = lax.dynamic_slice_in_dim(partial, feat * half, half, 1)
            give = lax.dynamic_slice_in_dim(partial, (1 - feat) * half, half, 1)
            piece = (keep + lax.ppermute(give, "feat", swap)).astype(jnp.bfloat16)
            mine = lax.dynamic_update_slice(mine, piece, (owner * count + first, 0))

    whole = jnp.zeros((total, width * n), jnp.bfloat16)
    squares = jnp.zeros((total,), jnp.float32)
    for arrived in walk(mine, n, order):
        for owner, first, block in arrived:
            other = lax.ppermute(block, "feat", swap)
            for part, at in ((block, feat), (other, 1 - feat)):
                whole = lax.dynamic_update_slice(whole, part, (first, owner * width + at * half))
                wide = part.astype(jnp.float32)
                squares = squares.at[first : first + part.shape[0]].add(jnp.sum(wide * wide, axis=1))
    lengths = jnp.sqrt(squares + epsilon)

    owned = count // 2
    devices = 2 * n
    group = max(1, 256 // owned)
    groups = devices // group
    columns = train_feats.shape[0]
    scores = jnp.zeros((owned, devices * columns), jnp.bfloat16)
    at_group, at_place = me // group, me % group
    for shift in [groups // 2] + [k for k in range(1, groups) if k != groups // 2] + [0]:
        target = (at_group + shift) % groups
        start = target * group * owned
        rows = lax.dynamic_slice_in_dim(whole, start, group * owned, 0)
        raw = lax.dot_general(rows, train_feats, (((1,), (1,)), ((), ())), preferred_element_type=jnp.float32)
        span = lax.dynamic_slice_in_dim(lengths, start, group * owned, 0)
        tile = (raw / span[:, None]).astype(jnp.bfloat16)
        for turn in range(group):
            pairs = []
            for i in range(devices):
                pairs.append((i, (i // group + shift) % groups * group + (i + turn) % group))
            block = lax.dynamic_slice_in_dim(tile, (at_place + turn) % group * owned, owned, 0)
            if shift or turn:
                block = lax.ppermute(block, ("rows", "feat"), pairs)
            source = (at_group - shift) % groups * group + (at_place - turn) % group
            scores = lax.dynamic_update_slice(scores, block, (0, source * columns))
    return scores


def solution(mesh):
    placed = (P("rows", "feat"), P(("corpus", "feat"), "rows"), P(("corpus", "rows", "feat"), None))
    return jax.shard_map(
        functools.partial(per_device, mesh.shape["rows"]),
        mesh=mesh,
        in_specs=placed,
        out_specs=P(("rows", "feat"), "corpus"),
        check_vma=False,
    )
```

```python
import functools

import jax
import jax.numpy as jnp
from jax import lax
from jax.experimental import pallas as pl
from jax.experimental.pallas import tpu as pltpu
from jax.sharding import PartitionSpec as P

epsilon = 1e-06


def snake(n):
    if n == 8:
        return (lambda r: jnp.where(r % 2 == 0, r // 2, n - 1 - r // 2),
                lambda p: jnp.where(p < n // 2, 2 * p, 2 * (n - 1 - p) + 1),
                [0, 2, 4, 6, 7, 5, 3, 1])
    return (lambda r: r), (lambda p: p), list(range(n))


def tile_rows(owners, shifts, span, where, *refs):
    n_near = 2 * (owners - 1)
    near, (top, top_other, bottom, bottom_other, train) = refs[:n_near], refs[n_near : n_near + 5]
    scores, left, held, lengths, piece_sems, train_sems = refs[n_near + 5 :]
    width = top.shape[1]
    upper = top.shape[0]
    tile = held.shape[1]
    steps = train.shape[0] // tile

    def stream(j):
        return pltpu.make_async_copy(train.at[pl.ds(pl.multiple_of(j * tile, tile), tile), :], held.at[j % 2], train_sems.at[j % 2])

    def lay(source, first, number, k):
        columns = pl.ds(pl.multiple_of(where[k] * width, width), width)
        return pltpu.make_async_copy(
            source.at[pl.ds(pl.multiple_of(first, span), span), :],
            left.at[pl.ds(number * span, span), columns],
            piece_sems.at[number, k],
        )

    stream(0).start()
    for number in range(len(shifts)):
        first = where[2 * owners + number] * span
        for k, piece in enumerate(near):
            lay(piece, first, number, k).start()

        @pl.when(first < upper)
        def _():
            lay(top, first, number, n_near).start()
            lay(top_other, first, number, n_near + 1).start()

        @pl.when(first >= upper)
        def _():
            lay(bottom, first - upper, number, n_near).start()
            lay(bottom_other, first - upper, number, n_near + 1).start()

    for number in range(len(shifts)):
        for k in range(2 * owners):
            lay(top, 0, number, k).wait()

    sums = 0.0
    for at in range(0, left.shape[1], 128):
        wide = left[:, at : at + 128].astype(jnp.float32)
        sums = sums + wide * wide
    lengths[...] = jnp.broadcast_to(jnp.sqrt(jnp.sum(sums, axis=1, keepdims=True) + epsilon), lengths.shape)

    def step(j, carry):
        @pl.when(j + 1 < steps)
        def _():
            stream(j + 1).start()

        stream(j).wait()
        across = (((1,), (1,)), ((), ()))
        if left.shape[0] < tile:
            raw = lax.dot_general(held[j % 2], left[...], across, preferred_element_type=jnp.float32).T
        else:
            raw = lax.dot_general(left[...], held[j % 2], across, preferred_element_type=jnp.float32)
        for at in range(0, tile, 128):
            columns = pl.ds(pl.multiple_of(j * tile + at, 128), 128)
            scores[:, columns] = (raw[:, at : at + 128] / lengths[...]).astype(scores.dtype)
        return carry

    lax.fori_loop(0, steps, step, 0)


def group_scores(near, far, where, targets, train_feats, span):
    owners = len(near) // 2 + 1
    columns, depth = train_feats.shape
    rows = span * len(targets)
    where = jnp.stack(list(where) + list(targets)).astype(jnp.int32)
    tile = 512
    anywhere = pl.BlockSpec(memory_space=pl.ANY)
    return pl.pallas_call(
        functools.partial(tile_rows, owners, tuple(range(len(targets))), span),
        out_shape=jax.ShapeDtypeStruct((rows, columns), jnp.bfloat16),
        in_specs=[pl.BlockSpec(memory_space=pltpu.SMEM)] + [anywhere] * (len(near) + len(far) + 1),
        out_specs=pl.BlockSpec(memory_space=pltpu.VMEM),
        scratch_shapes=[
            pltpu.VMEM((rows, depth), jnp.bfloat16),
            pltpu.VMEM((2, tile, depth), jnp.bfloat16),
            pltpu.VMEM((rows, 128), jnp.float32),
            pltpu.SemaphoreType.DMA((len(targets), 2 * owners)),
            pltpu.SemaphoreType.DMA((2,)),
        ],
        compiler_params=pltpu.CompilerParams(vmem_limit_bytes=VMEM_LIMIT),
        cost_estimate=pl.CostEstimate(flops=2 * rows * columns * depth, bytes_accessed=2 * columns * depth, transcendentals=0),
    )(where, *near, *far, train_feats)


VMEM_LIMIT = 58 * 2**20
IN_FLIGHT = 5


def per_device(n, queries, kernel, train_feats):
    to_place, to_owner, order = snake(n)
    ahead = [(order[i], order[(i + 1) % n]) for i in range(n)]
    back = [(b, a) for a, b in ahead]
    swap = [(0, 1), (1, 0)]
    row = lax.axis_index("rows")
    feat = lax.axis_index("feat")
    me = row * 2 + feat
    place = to_place(row)
    before = lambda step: to_owner((place + n - step) % n)
    after = lambda step: to_owner((place + step) % n)
    count = queries.shape[0]
    width = kernel.shape[1]
    half = width // 2
    total = count * n

    def product(block):
        partial = jnp.dot(block, kernel, preferred_element_type=jnp.float32)
        return (lax.dynamic_slice_in_dim(partial, feat * half, half, 1),
                lax.dynamic_slice_in_dim(partial, (1 - feat) * half, half, 1))

    blocks = [(row, queries)]
    forward = backward = queries
    for step in range(1, n // 2):
        forward = lax.ppermute(forward, "rows", ahead)
        backward = lax.ppermute(backward, "rows", back)
        blocks += [(before(step), forward), (after(step), backward)]
    top = lax.ppermute(forward[: count // 2], "rows", ahead)
    bottom = lax.ppermute(backward[count // 2 :], "rows", back)
    keep = jnp.zeros((total, half), jnp.float32)
    give = jnp.zeros((total, half), jnp.float32)
    for owner, block in blocks:
        a, b = product(block)
        keep = lax.dynamic_update_slice(keep, a, (owner * count, 0))
        give = lax.dynamic_update_slice(give, b, (owner * count, 0))
    mine = (keep + lax.ppermute(give, "feat", swap)).astype(jnp.bfloat16)
    a, b = product(jnp.concatenate([top, bottom]))
    mine = lax.dynamic_update_slice(
        mine, (a + lax.ppermute(b, "feat", swap)).astype(jnp.bfloat16), (before(n // 2) * count, 0)
    )

    near, where = [mine, lax.ppermute(mine, "feat", swap)], [me, row * 2 + 1 - feat]
    forward = backward = mine
    for step in range(1, n // 2):
        forward = lax.ppermute(forward, "rows", ahead)
        backward = lax.ppermute(backward, "rows", back)
        for owner, block in ((before(step), forward), (after(step), backward)):
            near += [block, lax.ppermute(block, "feat", swap)]
            where += [owner * 2 + feat, owner * 2 + 1 - feat]
    top = lax.ppermute(forward[: total // 2], "rows", ahead)
    bottom = lax.ppermute(backward[total // 2 :], "rows", back)
    far = [top, lax.ppermute(top, "feat", swap), bottom, lax.ppermute(bottom, "feat", swap)]
    where += [before(n // 2) * 2 + feat, before(n // 2) * 2 + 1 - feat]

    owned = count // 2
    devices = 2 * n
    columns = train_feats.shape[0]
    group = 256 // owned
    groups = devices // group
    span = group * owned
    at_group, at_place = me // group, me % group
    shifts = [groups // 2] + [k for k in range(1, groups) if k != groups // 2] + [0]
    target = lambda shift: (at_group + shift) % groups
    first = group_scores(near, far, where, [target(shifts[0])], train_feats, span)
    rest = group_scores(near, far, where, [target(k) for k in shifts[1:]], train_feats, span)
    scores = jnp.zeros((owned, devices * columns), jnp.bfloat16)
    order = [(0, turn) for turn in range(group)]
    for turn in range(group):
        order += [(number, turn) for number in range(1, groups)]
    going, sources = [], []
    for number, turn in order:
        shift = shifts[number]
        tiles, offset = (first, 0) if number == 0 else (rest, (number - 1) * span)
        block = lax.dynamic_slice_in_dim(tiles, offset + (at_place + turn) % group * owned, owned, 0)
        source = (at_group + groups - shift) % groups * group + (at_place + group - turn) % group
        if shift or turn:
            pairs = [(i, (i // group + shift) % groups * group + (i + turn) % group) for i in range(devices)]
            if len(going) >= IN_FLIGHT:
                block, going[-IN_FLIGHT] = lax.optimization_barrier((block, going[-IN_FLIGHT]))
            going.append(lax.ppermute(block, ("rows", "feat"), pairs))
            sources.append(source)
        else:
            own = (block, source)
    for block, source in [own] + list(zip(going, sources)):
        scores = lax.dynamic_update_slice(scores, block, (0, source * columns))
    return scores


def solution(mesh):
    placed = (P("rows", "feat"), P(("corpus", "feat"), "rows"), P(("corpus", "rows", "feat"), None))
    return jax.shard_map(
        functools.partial(per_device, mesh.shape["rows"]),
        mesh=mesh,
        in_specs=placed,
        out_specs=P(("rows", "feat"), "corpus"),
        check_vma=False,
    )
```

```python
import functools

import jax
import jax.numpy as jnp
from jax import lax
from jax.experimental import pallas as pl
from jax.experimental.pallas import tpu as pltpu
from jax.sharding import PartitionSpec as P

epsilon = 1e-06


def snake(n):
    if n == 8:
        return (lambda r: jnp.where(r % 2 == 0, r // 2, n - 1 - r // 2),
                lambda p: jnp.where(p < n // 2, 2 * p, 2 * (n - 1 - p) + 1),
                [0, 2, 4, 6, 7, 5, 3, 1])
    return (lambda r: r), (lambda p: p), list(range(n))


def tile_rows(owners, skip, shifts, span, where, *refs):
    n_near = 2 * (owners - 1)
    near, (top, top_other, bottom, bottom_other, train) = refs[:n_near], refs[n_near : n_near + 5]
    scores, left, held, lengths, piece_sems, train_sems = refs[n_near + 5 :]
    width = top.shape[1]
    upper = top.shape[0]
    tile = held.shape[1]
    steps = train.shape[0] // tile

    def stream(j):
        return pltpu.make_async_copy(train.at[pl.ds(pl.multiple_of(j * tile, tile), tile), :], held.at[j % 2], train_sems.at[j % 2])

    def lay(source, first, number, k):
        columns = pl.ds(pl.multiple_of(where[k] * width, width), width)
        return pltpu.make_async_copy(
            source.at[pl.ds(pl.multiple_of(first, span), span), :],
            left.at[pl.ds(number * span, span), columns],
            piece_sems.at[number, k],
        )

    stream(0).start()
    for number in range(len(shifts)):
        first = where[2 * owners + skip + number] * span
        for k, piece in enumerate(near):
            lay(piece, first, number, k).start()

        @pl.when(first < upper)
        def _():
            lay(top, first, number, n_near).start()
            lay(top_other, first, number, n_near + 1).start()

        @pl.when(first >= upper)
        def _():
            lay(bottom, first - upper, number, n_near).start()
            lay(bottom_other, first - upper, number, n_near + 1).start()

    for number in range(len(shifts)):
        for k in range(2 * owners):
            lay(top, 0, number, k).wait()

    sums = 0.0
    for at in range(0, left.shape[1], 128):
        wide = left[:, at : at + 128].astype(jnp.float32)
        sums = sums + wide * wide
    lengths[...] = jnp.broadcast_to(jnp.sqrt(jnp.sum(sums, axis=1, keepdims=True) + epsilon), lengths.shape)

    def step(j, carry):
        @pl.when(j + 1 < steps)
        def _():
            stream(j + 1).start()

        stream(j).wait()
        across = (((1,), (1,)), ((), ()))
        if left.shape[0] < tile:
            raw = lax.dot_general(held[j % 2], left[...], across, preferred_element_type=jnp.float32).T
        else:
            raw = lax.dot_general(left[...], held[j % 2], across, preferred_element_type=jnp.float32)
        for at in range(0, tile, 128):
            columns = pl.ds(pl.multiple_of(j * tile + at, 128), 128)
            scores[:, columns] = (raw[:, at : at + 128] / lengths[...]).astype(scores.dtype)
        return carry

    lax.fori_loop(0, steps, step, 0)


def some_columns(count, base, group_at, far, span, where, *refs):
    near, refs = refs[:count], refs[count:]
    if far:
        top, top_other, bottom, bottom_other, train, raw_in, squares_in = refs[:7]
        scores, left, held, before, sums, piece_sems, train_sems, in_sems = refs[7:]
    else:
        train, raw_out, squares_out, left, held, piece_sems, train_sems = refs
    total = count + (2 if far else 0)
    width = (near[0] if near else top).shape[1]
    tile = held.shape[1]
    steps = train.shape[0] // tile
    first = where[group_at] * span

    def stream(j, k):
        return pltpu.make_async_copy(
            train.at[pl.ds(pl.multiple_of(j * tile, tile), tile), pl.ds(pl.multiple_of(where[base + k] * width, width), width)],
            held.at[j % 2, :, pl.ds(k * width, width)],
            train_sems.at[j % 2, k],
        )

    def earlier(j):
        rows = pl.ds(pl.multiple_of(j * tile, tile), tile)
        return pltpu.make_async_copy(raw_in.at[rows, :], before.at[rows, :], in_sems.at[j])

    def lay(source, at, k):
        return pltpu.make_async_copy(
            source.at[pl.ds(pl.multiple_of(at, span), span), :], left.at[:, pl.ds(k * width, width)], piece_sems.at[k]
        )

    for k, piece in enumerate(near):
        lay(piece, first, k).start()
    if far:
        upper = top.shape[0]

        @pl.when(first < upper)
        def _():
            lay(top, first, count).start()
            lay(top_other, first, count + 1).start()

        @pl.when(first >= upper)
        def _():
            lay(bottom, first - upper, count).start()
            lay(bottom_other, first - upper, count + 1).start()

    for k in range(total):
        stream(0, k).start()
    if far:
        for j in range(steps):
            earlier(j).start()
    for k in range(total):
        lay(top if far else near[0], 0, k).wait()

    squared = squares_in[...] if far else 0.0
    for at in range(0, left.shape[1], 128):
        wide = left[:, at : at + 128].astype(jnp.float32)
        squared = squared + wide * wide
    if far:
        sums[...] = jnp.broadcast_to(jnp.sqrt(jnp.sum(squared, axis=1, keepdims=True) + epsilon), sums.shape)
    else:
        squares_out[...] = squared

    def step(j, carry):
        @pl.when(j + 1 < steps)
        def _():
            for k in range(total):
                stream(j + 1, k).start()

        for k in range(total):
            stream(j, k).wait()
        raw = lax.dot_general(held[j % 2], left[...], (((1,), (1,)), ((), ())), preferred_element_type=jnp.float32)
        rows = pl.ds(pl.multiple_of(j * tile, tile), tile)
        if not far:
            raw_out[rows, :] = raw
            return carry
        earlier(j).wait()
        raw = (before[rows, :] + raw).T
        for at in range(0, tile, 128):
            columns = pl.ds(pl.multiple_of(j * tile + at, 128), 128)
            scores[:, columns] = (raw[:, at : at + 128] / sums[...]).astype(scores.dtype)
        return carry

    lax.fori_loop(0, steps, step, 0)


def group_part(near, where, base, group_at, train_feats, span, far=(), earlier=()):
    columns = train_feats.shape[0]
    total = len(near) + len(far) // 2
    depth = total * (list(near) + list(far))[0].shape[1]
    tile = 512
    anywhere, inside = pl.BlockSpec(memory_space=pl.ANY), pl.BlockSpec(memory_space=pltpu.VMEM)
    in_specs = [pl.BlockSpec(memory_space=pltpu.SMEM)] + [anywhere] * (len(near) + len(far) + 1)
    scratch = [pltpu.VMEM((span, depth), jnp.bfloat16), pltpu.VMEM((2, tile, depth), jnp.bfloat16)]
    sems = [pltpu.SemaphoreType.DMA((total,)), pltpu.SemaphoreType.DMA((2, total))]
    if far:
        in_specs += [anywhere, inside]
        out_shape, out_specs = jax.ShapeDtypeStruct((span, columns), jnp.bfloat16), inside
        scratch += [pltpu.VMEM((columns, span), jnp.float32), pltpu.VMEM((span, 128), jnp.float32)]
        sems += [pltpu.SemaphoreType.DMA((columns // tile,))]
    else:
        out_shape = (jax.ShapeDtypeStruct((columns, span), jnp.float32), jax.ShapeDtypeStruct((span, 128), jnp.float32))
        out_specs = (inside, inside)
    return pl.pallas_call(
        functools.partial(some_columns, len(near), base, group_at, bool(far), span),
        out_shape=out_shape,
        in_specs=in_specs,
        out_specs=out_specs,
        scratch_shapes=scratch + sems,
        compiler_params=pltpu.CompilerParams(vmem_limit_bytes=VMEM_LIMIT),
        cost_estimate=pl.CostEstimate(flops=2 * span * columns * depth, bytes_accessed=2 * columns * depth, transcendentals=0),
    )(where, *near, *far, train_feats, *earlier)


def group_scores(near, far, where, skip, targets, train_feats, span):
    owners = len(near) // 2 + 1
    columns, depth = train_feats.shape
    rows = span * targets
    tile = 512
    anywhere = pl.BlockSpec(memory_space=pl.ANY)
    return pl.pallas_call(
        functools.partial(tile_rows, owners, skip, tuple(range(targets)), span),
        out_shape=jax.ShapeDtypeStruct((rows, columns), jnp.bfloat16),
        in_specs=[pl.BlockSpec(memory_space=pltpu.SMEM)] + [anywhere] * (len(near) + len(far) + 1),
        out_specs=pl.BlockSpec(memory_space=pltpu.VMEM),
        scratch_shapes=[
            pltpu.VMEM((rows, depth), jnp.bfloat16),
            pltpu.VMEM((2, tile, depth), jnp.bfloat16),
            pltpu.VMEM((rows, 128), jnp.float32),
            pltpu.SemaphoreType.DMA((targets, 2 * owners)),
            pltpu.SemaphoreType.DMA((2,)),
        ],
        compiler_params=pltpu.CompilerParams(vmem_limit_bytes=VMEM_LIMIT),
        cost_estimate=pl.CostEstimate(flops=2 * rows * columns * depth, bytes_accessed=2 * columns * depth, transcendentals=0),
    )(where, *near, *far, train_feats)


VMEM_LIMIT = 58 * 2**20
IN_FLIGHT = 5


def per_device(n, queries, kernel, train_feats):
    to_place, to_owner, order = snake(n)
    ahead = [(order[i], order[(i + 1) % n]) for i in range(n)]
    back = [(b, a) for a, b in ahead]
    swap = [(0, 1), (1, 0)]
    row = lax.axis_index("rows")
    feat = lax.axis_index("feat")
    me = row * 2 + feat
    place = to_place(row)
    before = lambda step: to_owner((place + n - step) % n)
    after = lambda step: to_owner((place + step) % n)
    count = queries.shape[0]
    width = kernel.shape[1]
    half = width // 2
    total = count * n

    def product(block):
        partial = jnp.dot(block, kernel, preferred_element_type=jnp.float32)
        return (lax.dynamic_slice_in_dim(partial, feat * half, half, 1),
                lax.dynamic_slice_in_dim(partial, (1 - feat) * half, half, 1))

    devices = 2 * n
    owned = count // 2
    columns = train_feats.shape[0]
    group = 256 // owned
    groups = devices // group
    span = group * owned
    at_group, at_place = me // group, me % group
    shifts = [groups // 2] + [k for k in range(1, groups) if k != groups // 2] + [0]

    table = [me, row * 2 + 1 - feat]
    for step in range(1, n // 2 + 1):
        for owner in (before(step), after(step))[: 1 if 2 * step == n else 2]:
            table += [owner * 2 + feat, owner * 2 + 1 - feat]
    table = jnp.stack(table + [(at_group + shift) % groups for shift in shifts]).astype(jnp.int32)

    blocks = [(row, queries)]
    forward = backward = queries
    for step in range(1, n // 2):
        forward = lax.ppermute(forward, "rows", ahead)
        backward = lax.ppermute(backward, "rows", back)
        blocks += [(before(step), forward), (after(step), backward)]
        if step == 1:
            forward, table = lax.optimization_barrier((forward, table))
    top = lax.ppermute(forward[: count // 2], "rows", ahead)
    bottom = lax.ppermute(backward[count // 2 :], "rows", back)
    keep = jnp.zeros((total, half), jnp.float32)
    give = jnp.zeros((total, half), jnp.float32)
    for owner, block in blocks:
        a, b = product(block)
        keep = lax.dynamic_update_slice(keep, a, (owner * count, 0))
        give = lax.dynamic_update_slice(give, b, (owner * count, 0))
    mine = (keep + lax.ppermute(give, "feat", swap)).astype(jnp.bfloat16)
    a, b = product(jnp.concatenate([top, bottom]))
    mine = lax.dynamic_update_slice(
        mine, (a + lax.ppermute(b, "feat", swap)).astype(jnp.bfloat16), (before(n // 2) * count, 0)
    )

    near = [mine, lax.ppermute(mine, "feat", swap)]
    forward = backward = mine
    for step in range(1, n // 2):
        forward = lax.ppermute(forward, "rows", ahead)
        backward = lax.ppermute(backward, "rows", back)
        if step == n // 2 - 1:
            early = len(near)
            partial = group_part(near, table, 0, devices, train_feats, span)
            forward, backward, squares = lax.optimization_barrier((forward, backward, partial[1]))
            partial = (partial[0], squares)
        for block in (forward, backward):
            near += [block, lax.ppermute(block, "feat", swap)]
    top = lax.ppermute(forward[: total // 2], "rows", ahead)
    bottom = lax.ppermute(backward[total // 2 :], "rows", back)
    far = [top, lax.ppermute(top, "feat", swap), bottom, lax.ppermute(bottom, "feat", swap)]

    first = group_part(near[early:], table, early, devices, train_feats, span, far, partial)
    rest = group_scores(near, far, table, 1, groups - 1, train_feats, span)
    scores = jnp.zeros((owned, devices * columns), jnp.bfloat16)
    order = [(0, turn) for turn in range(group)]
    for turn in range(group):
        order += [(number, turn) for number in range(1, groups)]
    going, sources = [], []
    for number, turn in order:
        shift = shifts[number]
        tiles, offset = (first, 0) if number == 0 else (rest, (number - 1) * span)
        block = lax.dynamic_slice_in_dim(tiles, offset + (at_place + turn) % group * owned, owned, 0)
        source = (at_group + groups - shift) % groups * group + (at_place + group - turn) % group
        if shift or turn:
            pairs = [(i, (i // group + shift) % groups * group + (i + turn) % group) for i in range(devices)]
            if len(going) >= IN_FLIGHT:
                block, going[-IN_FLIGHT] = lax.optimization_barrier((block, going[-IN_FLIGHT]))
            going.append(lax.ppermute(block, ("rows", "feat"), pairs))
            sources.append(source)
        else:
            own = (block, source)
    for block, source in [own] + list(zip(going, sources)):
        scores = lax.dynamic_update_slice(scores, block, (0, source * columns))
    return scores


def solution(mesh):
    placed = (P("rows", "feat"), P(("corpus", "feat"), "rows"), P(("corpus", "rows", "feat"), None))
    return jax.shard_map(
        functools.partial(per_device, mesh.shape["rows"]),
        mesh=mesh,
        in_specs=placed,
        out_specs=P(("rows", "feat"), "corpus"),
        check_vma=False,
    )
```

```python
import functools

import jax
import jax.numpy as jnp
from jax import lax
from jax.experimental import pallas as pl
from jax.experimental.pallas import tpu as pltpu
from jax.sharding import PartitionSpec as P

epsilon = 1e-06


def snake(n):
    if n == 8:
        return (lambda r: jnp.where(r % 2 == 0, r // 2, n - 1 - r // 2),
                lambda p: jnp.where(p < n // 2, 2 * p, 2 * (n - 1 - p) + 1),
                [0, 2, 4, 6, 7, 5, 3, 1])
    return (lambda r: r), (lambda p: p), list(range(n))


def tile_rows(owners, skip, shifts, span, where, *refs):
    n_near = 2 * (owners - 1)
    near, (top, top_other, bottom, bottom_other, train) = refs[:n_near], refs[n_near : n_near + 5]
    scores, left, held, lengths, piece_sems, train_sems = refs[n_near + 5 :]
    width = top.shape[1]
    upper = top.shape[0]
    tile = held.shape[1]
    steps = train.shape[0] // tile

    def stream(j):
        return pltpu.make_async_copy(train.at[pl.ds(pl.multiple_of(j * tile, tile), tile), :], held.at[j % 2], train_sems.at[j % 2])

    def lay(source, first, number, k):
        columns = pl.ds(pl.multiple_of(where[k] * width, width), width)
        return pltpu.make_async_copy(
            source.at[pl.ds(pl.multiple_of(first, span), span), :],
            left.at[pl.ds(number * span, span), columns],
            piece_sems.at[number, k],
        )

    stream(0).start()
    for number in range(len(shifts)):
        first = where[2 * owners + skip + number] * span
        for k, piece in enumerate(near):
            lay(piece, first, number, k).start()

        @pl.when(first < upper)
        def _():
            lay(top, first, number, n_near).start()
            lay(top_other, first, number, n_near + 1).start()

        @pl.when(first >= upper)
        def _():
            lay(bottom, first - upper, number, n_near).start()
            lay(bottom_other, first - upper, number, n_near + 1).start()

    for number in range(len(shifts)):
        for k in range(2 * owners):
            lay(top, 0, number, k).wait()

    sums = 0.0
    for at in range(0, left.shape[1], 128):
        wide = left[:, at : at + 128].astype(jnp.float32)
        sums = sums + wide * wide
    lengths[...] = jnp.broadcast_to(jnp.sqrt(jnp.sum(sums, axis=1, keepdims=True) + epsilon), lengths.shape)

    def step(j, carry):
        @pl.when(j + 1 < steps)
        def _():
            stream(j + 1).start()

        stream(j).wait()
        across = (((1,), (1,)), ((), ()))
        if left.shape[0] < tile:
            raw = lax.dot_general(held[j % 2], left[...], across, preferred_element_type=jnp.float32).T
        else:
            raw = lax.dot_general(left[...], held[j % 2], across, preferred_element_type=jnp.float32)
        for at in range(0, tile, 128):
            columns = pl.ds(pl.multiple_of(j * tile + at, 128), 128)
            scores[:, columns] = (raw[:, at : at + 128] / lengths[...]).astype(scores.dtype)
        return carry

    lax.fori_loop(0, steps, step, 0)


def some_columns(count, base, group_at, last, more, owned, where, *refs):
    near, refs = refs[: 4 if last else count], refs[4 if last else count :]
    train, refs = refs[0], refs[1:]
    if more:
        raw_in, squares_in, refs = refs[0], refs[1], refs[2:]
    if last:
        outs = refs[: len(refs) - (7 if more else 5)]
        refs = refs[len(outs) :]
    else:
        raw_out, squares_out, refs = refs[0], refs[1], refs[2:]
    left, held, piece_sems, train_sems = refs[:4]
    if more:
        before, in_sems = refs[4:6]
    span = left.shape[0]
    group = span // owned
    width = near[0].shape[1]
    tile = held.shape[1]
    steps = train.shape[0] // tile
    first = where[group_at] * span
    place = where[where.shape[0] - 1]

    def stream(j, k):
        return pltpu.make_async_copy(
            train.at[pl.ds(pl.multiple_of(j * tile, tile), tile), pl.ds(pl.multiple_of(where[base + k] * width, width), width)],
            held.at[j % 2, :, pl.ds(k * width, width)],
            train_sems.at[j % 2, k],
        )

    def earlier(j):
        columns = pl.ds(pl.multiple_of(j * tile, tile), tile)
        return pltpu.make_async_copy(raw_in.at[:, columns], before.at[:, columns], in_sems.at[j])

    def lay(source, start, k, turn):
        at = start + lax.rem(place + turn, group) * owned
        return pltpu.make_async_copy(
            source.at[pl.ds(pl.multiple_of(at, owned), owned), :],
            left.at[pl.ds(turn * owned, owned), pl.ds(k * width, width)],
            piece_sems.at[k, turn],
        )

    def lay_all(some, start):
        for k, piece in enumerate(some):
            for turn in range(group):
                lay(piece, start, k, turn).start()

    if last:
        upper = near[0].shape[0]
        pl.when(first < upper)(lambda: lay_all(near[:2], first))
        pl.when(first >= upper)(lambda: lay_all(near[2:], first - upper))
    else:
        lay_all(near, first)
    for k in range(count):
        stream(0, k).start()
    if more:
        for j in range(steps):
            earlier(j).start()
    for k in range(count):
        for turn in range(group):
            lay(near[0], 0, k, turn).wait()

    squared = squares_in[...] if more else 0.0
    for at in range(0, left.shape[1], 128):
        wide = left[:, at : at + 128].astype(jnp.float32)
        squared = squared + wide * wide
    if last:
        lengths = refs[-1]
        lengths[...] = jnp.broadcast_to(jnp.sqrt(jnp.sum(squared, axis=1, keepdims=True) + epsilon), lengths.shape)
    else:
        squares_out[...] = squared

    def step(j, carry):
        @pl.when(j + 1 < steps)
        def _():
            for k in range(count):
                stream(j + 1, k).start()

        for k in range(count):
            stream(j, k).wait()
        across = (((1,), (1,)), ((), ()))
        if last:
            raw = lax.dot_general(left[...], held[j % 2], across, preferred_element_type=jnp.float32)
        else:
            raw = lax.dot_general(held[j % 2], left[...], across, preferred_element_type=jnp.float32).T
        columns = pl.ds(pl.multiple_of(j * tile, tile), tile)
        if more:
            earlier(j).wait()
            raw = before[:, columns] + raw
        if not last:
            raw_out[:, columns] = raw
            return carry
        for at in range(0, tile, 128):
            part = (raw[:, at : at + 128] / lengths[...]).astype(outs[0].dtype)
            for turn in range(group):
                outs[turn][:, pl.ds(pl.multiple_of(j * tile + at, 128), 128)] = part[turn * owned : (turn + 1) * owned]
        return carry

    lax.fori_loop(0, steps, step, 0)


def group_part(pieces, table, base, group_at, train_feats, span, owned, earlier=(), last=False):
    columns = train_feats.shape[0]
    count = len(pieces) // 2 if last else len(pieces)
    depth = count * pieces[0].shape[1]
    tile = 512
    group = span // owned
    anywhere, inside = pl.BlockSpec(memory_space=pl.ANY), pl.BlockSpec(memory_space=pltpu.VMEM)
    in_specs = [pl.BlockSpec(memory_space=pltpu.SMEM)] + [anywhere] * (len(pieces) + 1)
    scratch = [
        pltpu.VMEM((span, depth), jnp.bfloat16),
        pltpu.VMEM((2, tile, depth), jnp.bfloat16),
        pltpu.SemaphoreType.DMA((count, group)),
        pltpu.SemaphoreType.DMA((2, count)),
    ]
    if earlier:
        in_specs += [anywhere, inside]
        scratch += [pltpu.VMEM((span, columns), jnp.float32), pltpu.SemaphoreType.DMA((columns // tile,))]
    if last:
        scratch += [pltpu.VMEM((span, 128), jnp.float32)]
        out_shape = (jax.ShapeDtypeStruct((owned, columns), jnp.bfloat16),) * group
        out_specs = (inside,) * group
    else:
        out_shape = (jax.ShapeDtypeStruct((span, columns), jnp.float32), jax.ShapeDtypeStruct((span, 128), jnp.float32))
        out_specs = (inside, inside)
    return pl.pallas_call(
        functools.partial(some_columns, count, base, group_at, last, bool(earlier), owned),
        out_shape=out_shape,
        in_specs=in_specs,
        out_specs=out_specs,
        scratch_shapes=scratch,
        compiler_params=pltpu.CompilerParams(vmem_limit_bytes=VMEM_LIMIT),
        cost_estimate=pl.CostEstimate(flops=2 * span * columns * depth, bytes_accessed=2 * columns * depth, transcendentals=0),
    )(table, *pieces, train_feats, *earlier)


def group_scores(near, far, where, skip, targets, train_feats, span):
    owners = len(near) // 2 + 1
    columns, depth = train_feats.shape
    rows = span * targets
    tile = 512
    anywhere = pl.BlockSpec(memory_space=pl.ANY)
    return pl.pallas_call(
        functools.partial(tile_rows, owners, skip, tuple(range(targets)), span),
        out_shape=jax.ShapeDtypeStruct((rows, columns), jnp.bfloat16),
        in_specs=[pl.BlockSpec(memory_space=pltpu.SMEM)] + [anywhere] * (len(near) + len(far) + 1),
        out_specs=pl.BlockSpec(memory_space=pltpu.VMEM),
        scratch_shapes=[
            pltpu.VMEM((rows, depth), jnp.bfloat16),
            pltpu.VMEM((2, tile, depth), jnp.bfloat16),
            pltpu.VMEM((rows, 128), jnp.float32),
            pltpu.SemaphoreType.DMA((targets, 2 * owners)),
            pltpu.SemaphoreType.DMA((2,)),
        ],
        compiler_params=pltpu.CompilerParams(vmem_limit_bytes=VMEM_LIMIT),
        cost_estimate=pl.CostEstimate(flops=2 * rows * columns * depth, bytes_accessed=2 * columns * depth, transcendentals=0),
    )(where, *near, *far, train_feats)


VMEM_LIMIT = 58 * 2**20
IN_FLIGHT = 5


def per_device(n, queries, kernel, train_feats):
    to_place, to_owner, order = snake(n)
    ahead = [(order[i], order[(i + 1) % n]) for i in range(n)]
    back = [(b, a) for a, b in ahead]
    swap = [(0, 1), (1, 0)]
    row = lax.axis_index("rows")
    feat = lax.axis_index("feat")
    me = row * 2 + feat
    place = to_place(row)
    before = lambda step: to_owner((place + n - step) % n)
    after = lambda step: to_owner((place + step) % n)
    count = queries.shape[0]
    width = kernel.shape[1]
    half = width // 2
    total = count * n

    def product(block):
        partial = jnp.dot(block, kernel, preferred_element_type=jnp.float32)
        return (lax.dynamic_slice_in_dim(partial, feat * half, half, 1),
                lax.dynamic_slice_in_dim(partial, (1 - feat) * half, half, 1))

    devices = 2 * n
    owned = count // 2
    columns = train_feats.shape[0]
    group = 256 // owned
    groups = devices // group
    span = group * owned
    at_group, at_place = me // group, me % group
    shifts = [groups // 2] + [k for k in range(1, groups) if k != groups // 2] + [0]

    table = [me, row * 2 + 1 - feat]
    for step in range(1, n // 2 + 1):
        for owner in (before(step), after(step))[: 1 if 2 * step == n else 2]:
            table += [owner * 2 + feat, owner * 2 + 1 - feat]
    table = jnp.stack(table + [(at_group + shift) % groups for shift in shifts] + [at_place]).astype(jnp.int32)

    blocks = [(row, queries)]
    forward = backward = queries
    for step in range(1, n // 2):
        forward = lax.ppermute(forward, "rows", ahead)
        backward = lax.ppermute(backward, "rows", back)
        blocks += [(before(step), forward), (after(step), backward)]
        if step == 1:
            forward, table = lax.optimization_barrier((forward, table))
    top = lax.ppermute(forward[: count // 2], "rows", ahead)
    bottom = lax.ppermute(backward[count // 2 :], "rows", back)
    keep = jnp.zeros((total, half), jnp.float32)
    give = jnp.zeros((total, half), jnp.float32)
    for owner, block in blocks:
        a, b = product(block)
        keep = lax.dynamic_update_slice(keep, a, (owner * count, 0))
        give = lax.dynamic_update_slice(give, b, (owner * count, 0))
    mine = (keep + lax.ppermute(give, "feat", swap)).astype(jnp.bfloat16)
    top, bottom, mine = lax.optimization_barrier((top, bottom, mine))
    a, b = product(jnp.concatenate([top, bottom]))
    mine = lax.dynamic_update_slice(
        mine, (a + lax.ppermute(b, "feat", swap)).astype(jnp.bfloat16), (before(n // 2) * count, 0)
    )

    near = [mine, lax.ppermute(mine, "feat", swap)]
    forward = backward = mine
    for step in range(1, n // 2):
        forward = lax.ppermute(forward, "rows", ahead)
        backward = lax.ppermute(backward, "rows", back)
        if step == n // 2 - 1:
            early = len(near)
            partial = group_part(near, table, 0, devices, train_feats, span, owned)
            forward, backward, squares = lax.optimization_barrier((forward, backward, partial[1]))
            partial = (partial[0], squares)
        for block in (forward, backward):
            near += [block, lax.ppermute(block, "feat", swap)]
    top = lax.ppermute(forward[: total // 2], "rows", ahead)
    bottom = lax.ppermute(backward[total // 2 :], "rows", back)
    partial = group_part(near[early:], table, early, devices, train_feats, span, owned, partial)
    top, bottom, squares = lax.optimization_barrier((top, bottom, partial[1]))
    partial = (partial[0], squares)
    far = [top, lax.ppermute(top, "feat", swap), bottom, lax.ppermute(bottom, "feat", swap)]

    first = group_part(far, table, len(near), devices, train_feats, span, owned, partial, last=True)
    rest = group_scores(near, far, table, 1, groups - 1, train_feats, span)
    scores = jnp.zeros((owned, devices * columns), jnp.bfloat16)
    order = [(0, turn) for turn in range(group)]
    for turn in range(group):
        order += [(number, turn) for number in range(1, groups)]
    going, sources = [], []
    for number, turn in order:
        shift = shifts[number]
        if number == 0:
            block = first[turn]
        else:
            block = lax.dynamic_slice_in_dim(rest, (number - 1) * span + (at_place + turn) % group * owned, owned, 0)
        source = (at_group + groups - shift) % groups * group + (at_place + group - turn) % group
        if shift or turn:
            pairs = [(i, (i // group + shift) % groups * group + (i + turn) % group) for i in range(devices)]
            if len(going) >= IN_FLIGHT:
                block, going[-IN_FLIGHT] = lax.optimization_barrier((block, going[-IN_FLIGHT]))
            going.append(lax.ppermute(block, ("rows", "feat"), pairs))
            sources.append(source)
        else:
            own = (block, source)
    for block, source in [own] + list(zip(going, sources)):
        scores = lax.dynamic_update_slice(scores, block, (0, source * columns))
    return scores


def solution(mesh):
    placed = (P("rows", "feat"), P(("corpus", "feat"), "rows"), P(("corpus", "rows", "feat"), None))
    return jax.shard_map(
        functools.partial(per_device, mesh.shape["rows"]),
        mesh=mesh,
        in_specs=placed,
        out_specs=P(("rows", "feat"), "corpus"),
        check_vma=False,
    )
```

```python
import functools

import jax
import jax.numpy as jnp
from jax import lax
from jax.experimental import pallas as pl
from jax.experimental.pallas import tpu as pltpu
from jax.sharding import PartitionSpec as P

epsilon = 1e-06


def snake(n):
    if n == 8:
        return (lambda r: jnp.where(r % 2 == 0, r // 2, n - 1 - r // 2),
                lambda p: jnp.where(p < n // 2, 2 * p, 2 * (n - 1 - p) + 1),
                [0, 2, 4, 6, 7, 5, 3, 1])
    return (lambda r: r), (lambda p: p), list(range(n))


def tile_rows(owners, skip, shifts, span, where, *refs):
    n_near = 2 * (owners - 1)
    near, (top, top_other, bottom, bottom_other, train) = refs[:n_near], refs[n_near : n_near + 5]
    scores, left, held, lengths, piece_sems, train_sems = refs[n_near + 5 :]
    width = top.shape[1]
    upper = top.shape[0]
    tile = held.shape[1]
    steps = train.shape[0] // tile

    def stream(j):
        return pltpu.make_async_copy(train.at[pl.ds(pl.multiple_of(j * tile, tile), tile), :], held.at[j % 2], train_sems.at[j % 2])

    def lay(source, first, number, k):
        columns = pl.ds(pl.multiple_of(where[k] * width, width), width)
        return pltpu.make_async_copy(
            source.at[pl.ds(pl.multiple_of(first, span), span), :],
            left.at[pl.ds(number * span, span), columns],
            piece_sems.at[number, k],
        )

    stream(0).start()
    for number in range(len(shifts)):
        first = where[2 * owners + skip + number] * span
        for k, piece in enumerate(near):
            lay(piece, first, number, k).start()

        @pl.when(first < upper)
        def _():
            lay(top, first, number, n_near).start()
            lay(top_other, first, number, n_near + 1).start()

        @pl.when(first >= upper)
        def _():
            lay(bottom, first - upper, number, n_near).start()
            lay(bottom_other, first - upper, number, n_near + 1).start()

    for number in range(len(shifts)):
        for k in range(2 * owners):
            lay(top, 0, number, k).wait()

    sums = 0.0
    for at in range(0, left.shape[1], 128):
        wide = left[:, at : at + 128].astype(jnp.float32)
        sums = sums + wide * wide
    lengths[...] = jnp.broadcast_to(jnp.sqrt(jnp.sum(sums, axis=1, keepdims=True) + epsilon), lengths.shape)

    def step(j, carry):
        @pl.when(j + 1 < steps)
        def _():
            stream(j + 1).start()

        stream(j).wait()
        across = (((1,), (1,)), ((), ()))
        if left.shape[0] < tile:
            raw = lax.dot_general(held[j % 2], left[...], across, preferred_element_type=jnp.float32).T
        else:
            raw = lax.dot_general(left[...], held[j % 2], across, preferred_element_type=jnp.float32)
        for at in range(0, tile, 128):
            columns = pl.ds(pl.multiple_of(j * tile + at, 128), 128)
            scores[:, columns] = (raw[:, at : at + 128] / lengths[...]).astype(scores.dtype)
        return carry

    lax.fori_loop(0, steps, step, 0)


def some_columns(count, base, group_at, last, more, owned, where, *refs):
    near, refs = refs[: 4 if last else count], refs[4 if last else count :]
    train, refs = refs[0], refs[1:]
    if more:
        raw_in, squares_in, refs = refs[0], refs[1], refs[2:]
    if last:
        outs = refs[: len(refs) - (7 if more else 5)]
        refs = refs[len(outs) :]
    else:
        raw_out, squares_out, refs = refs[0], refs[1], refs[2:]
    left, held, piece_sems, train_sems = refs[:4]
    if more:
        before, in_sems = refs[4:6]
    span = left.shape[0]
    group = span // owned
    width = near[0].shape[1]
    tile = held.shape[1]
    steps = train.shape[0] // tile
    first = where[group_at] * span
    place = where[where.shape[0] - 1]

    def stream(j, k):
        return pltpu.make_async_copy(
            train.at[pl.ds(pl.multiple_of(j * tile, tile), tile), pl.ds(pl.multiple_of(where[base + k] * width, width), width)],
            held.at[j % 2, :, pl.ds(k * width, width)],
            train_sems.at[j % 2, k],
        )

    def earlier(j):
        columns = pl.ds(pl.multiple_of(j * tile, tile), tile)
        return pltpu.make_async_copy(raw_in.at[:, columns], before.at[:, columns], in_sems.at[j])

    def lay(source, start, k, turn):
        at = start + lax.rem(place + turn, group) * owned
        return pltpu.make_async_copy(
            source.at[pl.ds(pl.multiple_of(at, owned), owned), :],
            left.at[pl.ds(turn * owned, owned), pl.ds(k * width, width)],
            piece_sems.at[k, turn],
        )

    def lay_all(some, start):
        for k, piece in enumerate(some):
            for turn in range(group):
                lay(piece, start, k, turn).start()

    if last:
        upper = near[0].shape[0]
        pl.when(first < upper)(lambda: lay_all(near[:2], first))
        pl.when(first >= upper)(lambda: lay_all(near[2:], first - upper))
    else:
        lay_all(near, first)
    for k in range(count):
        stream(0, k).start()
    if more:
        for j in range(steps):
            earlier(j).start()
    for k in range(count):
        for turn in range(group):
            lay(near[0], 0, k, turn).wait()

    squared = squares_in[...] if more else 0.0
    for at in range(0, left.shape[1], 128):
        wide = left[:, at : at + 128].astype(jnp.float32)
        squared = squared + wide * wide
    if last:
        lengths = refs[-1]
        lengths[...] = jnp.broadcast_to(jnp.sqrt(jnp.sum(squared, axis=1, keepdims=True) + epsilon), lengths.shape)
    else:
        squares_out[...] = squared

    def step(j, carry):
        @pl.when(j + 1 < steps)
        def _():
            for k in range(count):
                stream(j + 1, k).start()

        for k in range(count):
            stream(j, k).wait()
        across = (((1,), (1,)), ((), ()))
        if last:
            raw = lax.dot_general(left[...], held[j % 2], across, preferred_element_type=jnp.float32)
        else:
            raw = lax.dot_general(held[j % 2], left[...], across, preferred_element_type=jnp.float32).T
        columns = pl.ds(pl.multiple_of(j * tile, tile), tile)
        if more:
            earlier(j).wait()
            raw = before[:, columns] + raw
        if not last:
            raw_out[:, columns] = raw
            return carry
        for at in range(0, tile, 128):
            part = (raw[:, at : at + 128] / lengths[...]).astype(outs[0].dtype)
            for turn in range(group):
                outs[turn][:, pl.ds(pl.multiple_of(j * tile + at, 128), 128)] = part[turn * owned : (turn + 1) * owned]
        return carry

    lax.fori_loop(0, steps, step, 0)


def group_part(pieces, table, base, group_at, train_feats, span, owned, earlier=(), last=False):
    columns = train_feats.shape[0]
    count = len(pieces) // 2 if last else len(pieces)
    depth = count * pieces[0].shape[1]
    tile = 512
    group = span // owned
    anywhere, inside = pl.BlockSpec(memory_space=pl.ANY), pl.BlockSpec(memory_space=pltpu.VMEM)
    in_specs = [pl.BlockSpec(memory_space=pltpu.SMEM)] + [anywhere] * (len(pieces) + 1)
    scratch = [
        pltpu.VMEM((span, depth), jnp.bfloat16),
        pltpu.VMEM((2, tile, depth), jnp.bfloat16),
        pltpu.SemaphoreType.DMA((count, group)),
        pltpu.SemaphoreType.DMA((2, count)),
    ]
    if earlier:
        in_specs += [anywhere, inside]
        scratch += [pltpu.VMEM((span, columns), jnp.float32), pltpu.SemaphoreType.DMA((columns // tile,))]
    if last:
        scratch += [pltpu.VMEM((span, 128), jnp.float32)]
        out_shape = (jax.ShapeDtypeStruct((owned, columns), jnp.bfloat16),) * group
        out_specs = (inside,) * group
    else:
        out_shape = (jax.ShapeDtypeStruct((span, columns), jnp.float32), jax.ShapeDtypeStruct((span, 128), jnp.float32))
        out_specs = (inside, inside)
    return pl.pallas_call(
        functools.partial(some_columns, count, base, group_at, last, bool(earlier), owned),
        out_shape=out_shape,
        in_specs=in_specs,
        out_specs=out_specs,
        scratch_shapes=scratch,
        compiler_params=pltpu.CompilerParams(vmem_limit_bytes=VMEM_LIMIT),
        cost_estimate=pl.CostEstimate(flops=2 * span * columns * depth, bytes_accessed=2 * columns * depth, transcendentals=0),
    )(table, *pieces, train_feats, *earlier)


def group_scores(near, far, where, skip, targets, train_feats, span):
    owners = len(near) // 2 + 1
    columns, depth = train_feats.shape
    rows = span * targets
    tile = 512
    anywhere = pl.BlockSpec(memory_space=pl.ANY)
    return pl.pallas_call(
        functools.partial(tile_rows, owners, skip, tuple(range(targets)), span),
        out_shape=jax.ShapeDtypeStruct((rows, columns), jnp.bfloat16),
        in_specs=[pl.BlockSpec(memory_space=pltpu.SMEM)] + [anywhere] * (len(near) + len(far) + 1),
        out_specs=pl.BlockSpec(memory_space=pltpu.VMEM),
        scratch_shapes=[
            pltpu.VMEM((rows, depth), jnp.bfloat16),
            pltpu.VMEM((2, tile, depth), jnp.bfloat16),
            pltpu.VMEM((rows, 128), jnp.float32),
            pltpu.SemaphoreType.DMA((targets, 2 * owners)),
            pltpu.SemaphoreType.DMA((2,)),
        ],
        compiler_params=pltpu.CompilerParams(vmem_limit_bytes=VMEM_LIMIT),
        cost_estimate=pl.CostEstimate(flops=2 * rows * columns * depth, bytes_accessed=2 * columns * depth, transcendentals=0),
    )(where, *near, *far, train_feats)


VMEM_LIMIT = 58 * 2**20
IN_FLIGHT = 5


def per_device(n, queries, kernel, train_feats):
    to_place, to_owner, order = snake(n)
    ahead = [(order[i], order[(i + 1) % n]) for i in range(n)]
    back = [(b, a) for a, b in ahead]
    swap = [(0, 1), (1, 0)]
    row = lax.axis_index("rows")
    feat = lax.axis_index("feat")
    me = row * 2 + feat
    place = to_place(row)
    before = lambda step: to_owner((place + n - step) % n)
    after = lambda step: to_owner((place + step) % n)
    count = queries.shape[0]
    width = kernel.shape[1]
    half = width // 2
    total = count * n

    def product(block):
        partial = jnp.dot(block, kernel, preferred_element_type=jnp.float32)
        return (lax.dynamic_slice_in_dim(partial, feat * half, half, 1),
                lax.dynamic_slice_in_dim(partial, (1 - feat) * half, half, 1))

    devices = 2 * n
    owned = count // 2
    columns = train_feats.shape[0]
    group = 256 // owned
    groups = devices // group
    span = group * owned
    at_group, at_place = me // group, me % group
    shifts = [groups // 2] + [k for k in range(1, groups) if k != groups // 2] + [0]

    table = [me, row * 2 + 1 - feat]
    for step in range(1, n // 2 + 1):
        for owner in (before(step), after(step))[: 1 if 2 * step == n else 2]:
            table += [owner * 2 + feat, owner * 2 + 1 - feat]
    table = jnp.stack(table + [(at_group + shift) % groups for shift in shifts] + [at_place]).astype(jnp.int32)

    blocks = [(row, queries)]
    forward = backward = queries
    for step in range(1, n // 2):
        forward = lax.ppermute(forward, "rows", ahead)
        backward = lax.ppermute(backward, "rows", back)
        blocks += [(before(step), forward), (after(step), backward)]
        if step == 1:
            forward, table = lax.optimization_barrier((forward, table))
    top = lax.ppermute(forward[: count // 2], "rows", ahead)
    bottom = lax.ppermute(backward[count // 2 :], "rows", back)
    keep = jnp.zeros((total, half), jnp.float32)
    give = jnp.zeros((total, half), jnp.float32)
    for owner, block in blocks[:-2]:
        a, b = product(block)
        keep = lax.dynamic_update_slice(keep, a, (owner * count, 0))
        give = lax.dynamic_update_slice(give, b, (owner * count, 0))
    mine = (keep + lax.ppermute(give, "feat", swap)).astype(jnp.bfloat16)
    top, bottom, mine = lax.optimization_barrier((top, bottom, mine))
    late = [product(block) for _, block in blocks[-2:]] + [product(jnp.concatenate([top, bottom]))]
    here = jnp.concatenate([a for a, _ in late])
    there = lax.ppermute(jnp.concatenate([b for _, b in late]), "feat", swap)
    late = (here + there).astype(jnp.bfloat16)
    for k, owner in enumerate([owner for owner, _ in blocks[-2:]] + [before(n // 2)]):
        mine = lax.dynamic_update_slice(mine, late[k * count : (k + 1) * count], (owner * count, 0))

    near = [mine, lax.ppermute(mine, "feat", swap)]
    forward = backward = mine
    for step in range(1, n // 2):
        forward = lax.ppermute(forward, "rows", ahead)
        backward = lax.ppermute(backward, "rows", back)
        if step == n // 2 - 1:
            early = len(near)
            partial = group_part(near, table, 0, devices, train_feats, span, owned)
            forward, backward, squares = lax.optimization_barrier((forward, backward, partial[1]))
            partial = (partial[0], squares)
        for block in (forward, backward):
            near += [block, lax.ppermute(block, "feat", swap)]
    top = lax.ppermute(forward[: total // 2], "rows", ahead)
    bottom = lax.ppermute(backward[total // 2 :], "rows", back)
    partial = group_part(near[early:], table, early, devices, train_feats, span, owned, partial)
    top, bottom, squares = lax.optimization_barrier((top, bottom, partial[1]))
    partial = (partial[0], squares)
    far = [top, lax.ppermute(top, "feat", swap), bottom, lax.ppermute(bottom, "feat", swap)]

    first = group_part(far, table, len(near), devices, train_feats, span, owned, partial, last=True)
    rest = group_scores(near, far, table, 1, groups - 1, train_feats, span)
    scores = jnp.zeros((owned, devices * columns), jnp.bfloat16)
    order = [(0, turn) for turn in range(group)]
    for turn in range(group):
        order += [(number, turn) for number in (groups - 1, *range(1, groups - 1))]
    going, sources = [], []
    for number, turn in order:
        shift = shifts[number]
        if number == 0:
            block = first[turn]
        else:
            block = lax.dynamic_slice_in_dim(rest, (number - 1) * span + (at_place + turn) % group * owned, owned, 0)
        source = (at_group + groups - shift) % groups * group + (at_place + group - turn) % group
        if shift or turn:
            pairs = [(i, (i // group + shift) % groups * group + (i + turn) % group) for i in range(devices)]
            if len(going) >= IN_FLIGHT:
                block, going[-IN_FLIGHT] = lax.optimization_barrier((block, going[-IN_FLIGHT]))
            going.append(lax.ppermute(block, ("rows", "feat"), pairs))
            sources.append(source)
        else:
            own = (block, source)
    for block, source in [own] + list(zip(going, sources)):
        scores = lax.dynamic_update_slice(scores, block, (0, source * columns))
    return scores


def solution(mesh):
    placed = (P("rows", "feat"), P(("corpus", "feat"), "rows"), P(("corpus", "rows", "feat"), None))
    return jax.shard_map(
        functools.partial(per_device, mesh.shape["rows"]),
        mesh=mesh,
        in_specs=placed,
        out_specs=P(("rows", "feat"), "corpus"),
        check_vma=False,
    )
```

```python
import functools

import jax
import jax.numpy as jnp
from jax import lax
from jax.experimental import pallas as pl
from jax.experimental.pallas import tpu as pltpu
from jax.sharding import PartitionSpec as P

epsilon = 1e-06


def snake(n):
    if n == 8:
        return (lambda r: jnp.where(r % 2 == 0, r // 2, n - 1 - r // 2),
                lambda p: jnp.where(p < n // 2, 2 * p, 2 * (n - 1 - p) + 1),
                [0, 2, 4, 6, 7, 5, 3, 1])
    return (lambda r: r), (lambda p: p), list(range(n))


def tile_rows(owners, skip, shifts, span, where, *refs):
    n_near = 2 * (owners - 1)
    near, (top, top_other, bottom, bottom_other, train) = refs[:n_near], refs[n_near : n_near + 5]
    scores, left, held, lengths, piece_sems, train_sems = refs[n_near + 5 :]
    width = top.shape[1]
    upper = top.shape[0]
    tile = held.shape[1]
    steps = train.shape[0] // tile

    def stream(j):
        return pltpu.make_async_copy(train.at[pl.ds(pl.multiple_of(j * tile, tile), tile), :], held.at[j % 2], train_sems.at[j % 2])

    def lay(source, first, number, k):
        columns = pl.ds(pl.multiple_of(where[k] * width, width), width)
        return pltpu.make_async_copy(
            source.at[pl.ds(pl.multiple_of(first, span), span), :],
            left.at[pl.ds(number * span, span), columns],
            piece_sems.at[number, k],
        )

    stream(0).start()
    for number in range(len(shifts)):
        first = where[2 * owners + skip + number] * span
        for k, piece in enumerate(near):
            lay(piece, first, number, k).start()

        @pl.when(first < upper)
        def _():
            lay(top, first, number, n_near).start()
            lay(top_other, first, number, n_near + 1).start()

        @pl.when(first >= upper)
        def _():
            lay(bottom, first - upper, number, n_near).start()
            lay(bottom_other, first - upper, number, n_near + 1).start()

    for number in range(len(shifts)):
        for k in range(2 * owners):
            lay(top, 0, number, k).wait()

    sums = 0.0
    for at in range(0, left.shape[1], 128):
        wide = left[:, at : at + 128].astype(jnp.float32)
        sums = sums + wide * wide
    lengths[...] = jnp.broadcast_to(jnp.sqrt(jnp.sum(sums, axis=1, keepdims=True) + epsilon), lengths.shape)

    def step(j, carry):
        @pl.when(j + 1 < steps)
        def _():
            stream(j + 1).start()

        stream(j).wait()
        across = (((1,), (1,)), ((), ()))
        if left.shape[0] < tile:
            raw = lax.dot_general(held[j % 2], left[...], across, preferred_element_type=jnp.float32).T
        else:
            raw = lax.dot_general(left[...], held[j % 2], across, preferred_element_type=jnp.float32)
        for at in range(0, tile, 128):
            columns = pl.ds(pl.multiple_of(j * tile + at, 128), 128)
            scores[:, columns] = (raw[:, at : at + 128] / lengths[...]).astype(scores.dtype)
        return carry

    lax.fori_loop(0, steps, step, 0)


def some_columns(count, base, group_at, last, more, owned, where, *refs):
    near, refs = refs[: 4 if last else count], refs[4 if last else count :]
    train, refs = refs[0], refs[1:]
    if more:
        raw_in, squares_in, refs = refs[0], refs[1], refs[2:]
    if last:
        outs = refs[: len(refs) - (7 if more else 5)]
        refs = refs[len(outs) :]
    else:
        raw_out, squares_out, refs = refs[0], refs[1], refs[2:]
    left, held, piece_sems, train_sems = refs[:4]
    if more:
        before, in_sems = refs[4:6]
    span = left.shape[0]
    group = span // owned
    width = near[0].shape[1]
    tile = held.shape[1]
    steps = train.shape[0] // tile
    first = where[group_at] * span
    place = where[where.shape[0] - 1]

    def stream(j, pair):
        columns = pl.ds(pl.multiple_of(where[base + 2 * pair] // 2 * (2 * width), 2 * width), 2 * width)
        return pltpu.make_async_copy(
            train.at[pl.ds(pl.multiple_of(j * tile, tile), tile), columns],
            held.at[j, :, pl.ds(pair * 2 * width, 2 * width)],
            train_sems.at[j, pair],
        )

    def earlier(j):
        columns = pl.ds(pl.multiple_of(j * tile, tile), tile)
        return pltpu.make_async_copy(raw_in.at[:, columns], before.at[:, columns], in_sems.at[j])

    def lay(source, start, k, turn):
        at = start + lax.rem(place + turn, group) * owned
        return pltpu.make_async_copy(
            source.at[pl.ds(pl.multiple_of(at, owned), owned), :],
            left.at[pl.ds(turn * owned, owned), pl.ds(pl.multiple_of(k // 2 * (2 * width) + where[base + k] % 2 * width, width), width)],
            piece_sems.at[k, turn],
        )

    def lay_all(some, start):
        for k, piece in enumerate(some):
            for turn in range(group):
                lay(piece, start, k, turn).start()

    for pair in range(count // 2):
        stream(0, pair).start()
    if last:
        upper = near[0].shape[0]
        pl.when(first < upper)(lambda: lay_all(near[:2], first))
        pl.when(first >= upper)(lambda: lay_all(near[2:], first - upper))
    else:
        lay_all(near, first)
    for j in range(1, steps):
        for pair in range(count // 2):
            stream(j, pair).start()
    if more:
        for j in range(steps):
            earlier(j).start()
    for k in range(count):
        for turn in range(group):
            lay(near[0], 0, k, turn).wait()

    squared = squares_in[...] if more else 0.0
    for at in range(0, left.shape[1], 128):
        wide = left[:, at : at + 128].astype(jnp.float32)
        squared = squared + wide * wide
    if last:
        lengths = refs[-1]
        lengths[...] = jnp.broadcast_to(jnp.sqrt(jnp.sum(squared, axis=1, keepdims=True) + epsilon), lengths.shape)
    else:
        squares_out[...] = squared

    def step(j, carry):
        for pair in range(count // 2):
            stream(j, pair).wait()
        across = (((1,), (1,)), ((), ()))
        raw = lax.dot_general(left[...], held[j], across, preferred_element_type=jnp.float32)
        columns = pl.ds(pl.multiple_of(j * tile, tile), tile)
        if more:
            earlier(j).wait()
            raw = before[:, columns] + raw
        if not last:
            raw_out[:, columns] = raw
            return carry
        for at in range(0, tile, 128):
            part = (raw[:, at : at + 128] / lengths[...]).astype(outs[0].dtype)
            for turn in range(group):
                outs[turn][:, pl.ds(pl.multiple_of(j * tile + at, 128), 128)] = part[turn * owned : (turn + 1) * owned]
        return carry

    lax.fori_loop(0, steps, step, 0)


def group_part(pieces, table, base, group_at, train_feats, span, owned, earlier=(), last=False):
    columns = train_feats.shape[0]
    count = len(pieces) // 2 if last else len(pieces)
    depth = count * pieces[0].shape[1]
    tile = 512
    group = span // owned
    anywhere, inside = pl.BlockSpec(memory_space=pl.ANY), pl.BlockSpec(memory_space=pltpu.VMEM)
    in_specs = [pl.BlockSpec(memory_space=pltpu.SMEM)] + [anywhere] * (len(pieces) + 1)
    scratch = [
        pltpu.VMEM((span, depth), jnp.bfloat16),
        pltpu.VMEM((columns // tile, tile, depth), jnp.bfloat16),
        pltpu.SemaphoreType.DMA((count, group)),
        pltpu.SemaphoreType.DMA((columns // tile, count // 2)),
    ]
    if earlier:
        in_specs += [anywhere, inside]
        scratch += [pltpu.VMEM((span, columns), jnp.float32), pltpu.SemaphoreType.DMA((columns // tile,))]
    if last:
        scratch += [pltpu.VMEM((span, 128), jnp.float32)]
        out_shape = (jax.ShapeDtypeStruct((owned, columns), jnp.bfloat16),) * group
        out_specs = (inside,) * group
    else:
        out_shape = (jax.ShapeDtypeStruct((span, columns), jnp.float32), jax.ShapeDtypeStruct((span, 128), jnp.float32))
        out_specs = (inside, inside)
    return pl.pallas_call(
        functools.partial(some_columns, count, base, group_at, last, bool(earlier), owned),
        out_shape=out_shape,
        in_specs=in_specs,
        out_specs=out_specs,
        scratch_shapes=scratch,
        compiler_params=pltpu.CompilerParams(vmem_limit_bytes=VMEM_LIMIT),
        cost_estimate=pl.CostEstimate(flops=2 * span * columns * depth, bytes_accessed=2 * columns * depth, transcendentals=0),
    )(table, *pieces, train_feats, *earlier)


def group_scores(near, far, where, skip, targets, train_feats, span):
    owners = len(near) // 2 + 1
    columns, depth = train_feats.shape
    rows = span * targets
    tile = 512
    anywhere = pl.BlockSpec(memory_space=pl.ANY)
    return pl.pallas_call(
        functools.partial(tile_rows, owners, skip, tuple(range(targets)), span),
        out_shape=jax.ShapeDtypeStruct((rows, columns), jnp.bfloat16),
        in_specs=[pl.BlockSpec(memory_space=pltpu.SMEM)] + [anywhere] * (len(near) + len(far) + 1),
        out_specs=pl.BlockSpec(memory_space=pltpu.VMEM),
        scratch_shapes=[
            pltpu.VMEM((rows, depth), jnp.bfloat16),
            pltpu.VMEM((2, tile, depth), jnp.bfloat16),
            pltpu.VMEM((rows, 128), jnp.float32),
            pltpu.SemaphoreType.DMA((targets, 2 * owners)),
            pltpu.SemaphoreType.DMA((2,)),
        ],
        compiler_params=pltpu.CompilerParams(vmem_limit_bytes=VMEM_LIMIT),
        cost_estimate=pl.CostEstimate(flops=2 * rows * columns * depth, bytes_accessed=2 * columns * depth, transcendentals=0),
    )(where, *near, *far, train_feats)


VMEM_LIMIT = 58 * 2**20
IN_FLIGHT = 5


def per_device(n, queries, kernel, train_feats):
    to_place, to_owner, order = snake(n)
    ahead = [(order[i], order[(i + 1) % n]) for i in range(n)]
    back = [(b, a) for a, b in ahead]
    swap = [(0, 1), (1, 0)]
    row = lax.axis_index("rows")
    feat = lax.axis_index("feat")
    me = row * 2 + feat
    place = to_place(row)
    before = lambda step: to_owner((place + n - step) % n)
    after = lambda step: to_owner((place + step) % n)
    count = queries.shape[0]
    width = kernel.shape[1]
    half = width // 2
    total = count * n

    def product(block):
        partial = jnp.dot(block, kernel, preferred_element_type=jnp.float32)
        return (lax.dynamic_slice_in_dim(partial, feat * half, half, 1),
                lax.dynamic_slice_in_dim(partial, (1 - feat) * half, half, 1))

    devices = 2 * n
    owned = count // 2
    columns = train_feats.shape[0]
    group = 256 // owned
    groups = devices // group
    span = group * owned
    at_group, at_place = me // group, me % group
    shifts = [groups // 2] + [k for k in range(1, groups) if k != groups // 2] + [0]

    table = [me, row * 2 + 1 - feat]
    for step in range(1, n // 2 + 1):
        for owner in (before(step), after(step))[: 1 if 2 * step == n else 2]:
            table += [owner * 2 + feat, owner * 2 + 1 - feat]
    table = jnp.stack(table + [(at_group + shift) % groups for shift in shifts] + [at_place]).astype(jnp.int32)

    blocks = [(row, queries)]
    forward = backward = queries
    for step in range(1, n // 2):
        forward = lax.ppermute(forward, "rows", ahead)
        backward = lax.ppermute(backward, "rows", back)
        blocks += [(before(step), forward), (after(step), backward)]
        if step == 1:
            forward, table = lax.optimization_barrier((forward, table))
    top = lax.ppermute(forward[: count // 2], "rows", ahead)
    bottom = lax.ppermute(backward[count // 2 :], "rows", back)
    keep = jnp.zeros((total, half), jnp.float32)
    give = jnp.zeros((total, half), jnp.float32)
    for owner, block in blocks[:-2]:
        a, b = product(block)
        keep = lax.dynamic_update_slice(keep, a, (owner * count, 0))
        give = lax.dynamic_update_slice(give, b, (owner * count, 0))
    mine = (keep + lax.ppermute(give, "feat", swap)).astype(jnp.bfloat16)
    top, bottom, mine = lax.optimization_barrier((top, bottom, mine))
    late = [product(block) for _, block in blocks[-2:]] + [product(jnp.concatenate([top, bottom]))]
    here = jnp.concatenate([a for a, _ in late])
    there = lax.ppermute(jnp.concatenate([b for _, b in late]), "feat", swap)
    late = (here + there).astype(jnp.bfloat16)
    for k, owner in enumerate([owner for owner, _ in blocks[-2:]] + [before(n // 2)]):
        mine = lax.dynamic_update_slice(mine, late[k * count : (k + 1) * count], (owner * count, 0))

    near = [mine, lax.ppermute(mine, "feat", swap)]
    forward = backward = mine
    for step in range(1, n // 2):
        forward = lax.ppermute(forward, "rows", ahead)
        backward = lax.ppermute(backward, "rows", back)
        if step == n // 2 - 1:
            early = len(near)
            partial = group_part(near, table, 0, devices, train_feats, span, owned)
            forward, backward, squares = lax.optimization_barrier((forward, backward, partial[1]))
            partial = (partial[0], squares)
        for block in (forward, backward):
            near += [block, lax.ppermute(block, "feat", swap)]
    top = lax.ppermute(forward[: total // 2], "rows", ahead)
    bottom = lax.ppermute(backward[total // 2 :], "rows", back)
    partial = group_part(near[early:], table, early, devices, train_feats, span, owned, partial)
    top, bottom, squares = lax.optimization_barrier((top, bottom, partial[1]))
    partial = (partial[0], squares)
    far = [top, lax.ppermute(top, "feat", swap), bottom, lax.ppermute(bottom, "feat", swap)]

    first = group_part(far, table, len(near), devices, train_feats, span, owned, partial, last=True)
    rest = group_scores(near, far, table, 1, groups - 1, train_feats, span)
    scores = jnp.zeros((owned, devices * columns), jnp.bfloat16)
    order = [(0, turn) for turn in range(group)]
    for turn in range(group):
        order += [(number, turn) for number in (groups - 1, *range(1, groups - 1))]
    going, sources = [], []
    for number, turn in order:
        shift = shifts[number]
        if number == 0:
            block = first[turn]
        else:
            block = lax.dynamic_slice_in_dim(rest, (number - 1) * span + (at_place + turn) % group * owned, owned, 0)
        source = (at_group + groups - shift) % groups * group + (at_place + group - turn) % group
        if shift or turn:
            pairs = [(i, (i // group + shift) % groups * group + (i + turn) % group) for i in range(devices)]
            if len(going) >= IN_FLIGHT:
                block, going[-IN_FLIGHT] = lax.optimization_barrier((block, going[-IN_FLIGHT]))
            going.append(lax.ppermute(block, ("rows", "feat"), pairs))
            sources.append(source)
        else:
            own = (block, source)
    for block, source in [own] + list(zip(going, sources)):
        scores = lax.dynamic_update_slice(scores, block, (0, source * columns))
    return scores


def solution(mesh):
    placed = (P("rows", "feat"), P(("corpus", "feat"), "rows"), P(("corpus", "rows", "feat"), None))
    return jax.shard_map(
        functools.partial(per_device, mesh.shape["rows"]),
        mesh=mesh,
        in_specs=placed,
        out_specs=P(("rows", "feat"), "corpus"),
        check_vma=False,
    )
```

```python
import functools

import jax
import jax.numpy as jnp
from jax import lax
from jax.experimental import pallas as pl
from jax.experimental.pallas import tpu as pltpu
from jax.sharding import PartitionSpec as P

epsilon = 1e-06


def snake(n):
    if n == 8:
        return (lambda r: jnp.where(r % 2 == 0, r // 2, n - 1 - r // 2),
                lambda p: jnp.where(p < n // 2, 2 * p, 2 * (n - 1 - p) + 1),
                [0, 2, 4, 6, 7, 5, 3, 1])
    return (lambda r: r), (lambda p: p), list(range(n))


def tile_rows(owners, skip, shifts, span, where, *refs):
    n_near = 2 * (owners - 1)
    near, (top, top_other, bottom, bottom_other, train) = refs[:n_near], refs[n_near : n_near + 5]
    scores, left, held, lengths, piece_sems, train_sems = refs[n_near + 5 :]
    width = top.shape[1]
    upper = top.shape[0]
    tile = held.shape[1]
    steps = train.shape[0] // tile

    def stream(j):
        return pltpu.make_async_copy(train.at[pl.ds(pl.multiple_of(j * tile, tile), tile), :], held.at[j % 2], train_sems.at[j % 2])

    def lay(source, first, number, k):
        columns = pl.ds(pl.multiple_of(where[k] * width, width), width)
        return pltpu.make_async_copy(
            source.at[pl.ds(pl.multiple_of(first, span), span), :],
            left.at[pl.ds(number * span, span), columns],
            piece_sems.at[number, k],
        )

    stream(0).start()
    for number in range(len(shifts)):
        first = where[2 * owners + skip + number] * span
        for k, piece in enumerate(near):
            lay(piece, first, number, k).start()

        @pl.when(first < upper)
        def _():
            lay(top, first, number, n_near).start()
            lay(top_other, first, number, n_near + 1).start()

        @pl.when(first >= upper)
        def _():
            lay(bottom, first - upper, number, n_near).start()
            lay(bottom_other, first - upper, number, n_near + 1).start()

    for number in range(len(shifts)):
        for k in range(2 * owners):
            lay(top, 0, number, k).wait()

    sums = 0.0
    for at in range(0, left.shape[1], 128):
        wide = left[:, at : at + 128].astype(jnp.float32)
        sums = sums + wide * wide
    lengths[...] = jnp.broadcast_to(jnp.sqrt(jnp.sum(sums, axis=1, keepdims=True) + epsilon), lengths.shape)

    def step(j, carry):
        @pl.when(j + 1 < steps)
        def _():
            stream(j + 1).start()

        stream(j).wait()
        across = (((1,), (1,)), ((), ()))
        if left.shape[0] < tile:
            raw = lax.dot_general(held[j % 2], left[...], across, preferred_element_type=jnp.float32).T
        else:
            raw = lax.dot_general(left[...], held[j % 2], across, preferred_element_type=jnp.float32)
        for at in range(0, tile, 128):
            columns = pl.ds(pl.multiple_of(j * tile + at, 128), 128)
            scores[:, columns] = (raw[:, at : at + 128] / lengths[...]).astype(scores.dtype)
        return carry

    lax.fori_loop(0, steps, step, 0)


def some_columns(count, base, group_at, last, more, owned, where, *refs):
    near, refs = refs[: 4 if last else count], refs[4 if last else count :]
    train, refs = refs[0], refs[1:]
    if more:
        raw_in, squares_in, refs = refs[0], refs[1], refs[2:]
    if last:
        outs = refs[: len(refs) - (7 if more else 5)]
        refs = refs[len(outs) :]
    else:
        raw_out, squares_out, refs = refs[0], refs[1], refs[2:]
    left, held, piece_sems, train_sems = refs[:4]
    if more:
        before, in_sems = refs[4:6]
    span = left.shape[0]
    group = span // owned
    width = near[0].shape[1]
    tile = held.shape[1]
    steps = train.shape[0] // tile
    first = where[group_at] * span
    place = where[where.shape[0] - 1]

    def stream(j, pair):
        columns = pl.ds(pl.multiple_of(where[base + 2 * pair] // 2 * (2 * width), 2 * width), 2 * width)
        return pltpu.make_async_copy(
            train.at[pl.ds(pl.multiple_of(j * tile, tile), tile), columns],
            held.at[j, :, pl.ds(pair * 2 * width, 2 * width)],
            train_sems.at[j, pair],
        )

    def earlier(j):
        columns = pl.ds(pl.multiple_of(j * tile, tile), tile)
        return pltpu.make_async_copy(raw_in.at[:, columns], before.at[:, columns], in_sems.at[j])

    def lay(source, start, k, turn):
        at = start + lax.rem(place + turn, group) * owned
        return pltpu.make_async_copy(
            source.at[pl.ds(pl.multiple_of(at, owned), owned), :],
            left.at[pl.ds(turn * owned, owned), pl.ds(pl.multiple_of(k // 2 * (2 * width) + where[base + k] % 2 * width, width), width)],
            piece_sems.at[k, turn],
        )

    def lay_all(some, start):
        for k, piece in enumerate(some):
            for turn in range(group):
                lay(piece, start, k, turn).start()

    for pair in range(count // 2):
        stream(0, pair).start()
    if last:
        upper = near[0].shape[0]
        pl.when(first < upper)(lambda: lay_all(near[:2], first))
        pl.when(first >= upper)(lambda: lay_all(near[2:], first - upper))
    else:
        lay_all(near, first)
    for j in range(1, steps):
        for pair in range(count // 2):
            stream(j, pair).start()
    if more:
        for j in range(steps):
            earlier(j).start()
    for k in range(count):
        for turn in range(group):
            lay(near[0], 0, k, turn).wait()

    squared = squares_in[...] if more else 0.0
    for at in range(0, left.shape[1], 128):
        wide = left[:, at : at + 128].astype(jnp.float32)
        squared = squared + wide * wide
    if last:
        lengths = refs[-1]
        lengths[...] = jnp.broadcast_to(jnp.sqrt(jnp.sum(squared, axis=1, keepdims=True) + epsilon), lengths.shape)
    else:
        squares_out[...] = squared

    def step(j, carry):
        for pair in range(count // 2):
            stream(j, pair).wait()
        across = (((1,), (1,)), ((), ()))
        raw = lax.dot_general(left[...], held[j], across, preferred_element_type=jnp.float32)
        columns = pl.ds(pl.multiple_of(j * tile, tile), tile)
        if more:
            earlier(j).wait()
            raw = before[:, columns] + raw
        if not last:
            raw_out[:, columns] = raw
            return carry
        for at in range(0, tile, 128):
            part = (raw[:, at : at + 128] / lengths[...]).astype(outs[0].dtype)
            for turn in range(group):
                outs[turn][:, pl.ds(pl.multiple_of(j * tile + at, 128), 128)] = part[turn * owned : (turn + 1) * owned]
        return carry

    lax.fori_loop(0, steps, step, 0)


def group_part(pieces, table, base, group_at, train_feats, span, owned, earlier=(), last=False):
    columns = train_feats.shape[0]
    count = len(pieces) // 2 if last else len(pieces)
    depth = count * pieces[0].shape[1]
    tile = 512
    group = span // owned
    anywhere, inside = pl.BlockSpec(memory_space=pl.ANY), pl.BlockSpec(memory_space=pltpu.VMEM)
    in_specs = [pl.BlockSpec(memory_space=pltpu.SMEM)] + [anywhere] * (len(pieces) + 1)
    scratch = [
        pltpu.VMEM((span, depth), jnp.bfloat16),
        pltpu.VMEM((columns // tile, tile, depth), jnp.bfloat16),
        pltpu.SemaphoreType.DMA((count, group)),
        pltpu.SemaphoreType.DMA((columns // tile, count // 2)),
    ]
    if earlier:
        in_specs += [anywhere, inside]
        scratch += [pltpu.VMEM((span, columns), jnp.float32), pltpu.SemaphoreType.DMA((columns // tile,))]
    if last:
        scratch += [pltpu.VMEM((span, 128), jnp.float32)]
        out_shape = (jax.ShapeDtypeStruct((owned, columns), jnp.bfloat16),) * group
        out_specs = (inside,) * group
    else:
        out_shape = (jax.ShapeDtypeStruct((span, columns), jnp.float32), jax.ShapeDtypeStruct((span, 128), jnp.float32))
        out_specs = (inside, inside)
    return pl.pallas_call(
        functools.partial(some_columns, count, base, group_at, last, bool(earlier), owned),
        out_shape=out_shape,
        in_specs=in_specs,
        out_specs=out_specs,
        scratch_shapes=scratch,
        compiler_params=pltpu.CompilerParams(vmem_limit_bytes=VMEM_LIMIT),
        cost_estimate=pl.CostEstimate(flops=2 * span * columns * depth, bytes_accessed=2 * columns * depth, transcendentals=0),
    )(table, *pieces, train_feats, *earlier)


def group_scores(near, far, where, skip, targets, train_feats, span):
    owners = len(near) // 2 + 1
    columns, depth = train_feats.shape
    rows = span * targets
    tile = 512
    anywhere = pl.BlockSpec(memory_space=pl.ANY)
    return pl.pallas_call(
        functools.partial(tile_rows, owners, skip, tuple(range(targets)), span),
        out_shape=jax.ShapeDtypeStruct((rows, columns), jnp.bfloat16),
        in_specs=[pl.BlockSpec(memory_space=pltpu.SMEM)] + [anywhere] * (len(near) + len(far) + 1),
        out_specs=pl.BlockSpec(memory_space=pltpu.VMEM),
        scratch_shapes=[
            pltpu.VMEM((rows, depth), jnp.bfloat16),
            pltpu.VMEM((2, tile, depth), jnp.bfloat16),
            pltpu.VMEM((rows, 128), jnp.float32),
            pltpu.SemaphoreType.DMA((targets, 2 * owners)),
            pltpu.SemaphoreType.DMA((2,)),
        ],
        compiler_params=pltpu.CompilerParams(vmem_limit_bytes=VMEM_LIMIT),
        cost_estimate=pl.CostEstimate(flops=2 * rows * columns * depth, bytes_accessed=2 * columns * depth, transcendentals=0),
    )(where, *near, *far, train_feats)


VMEM_LIMIT = 58 * 2**20
IN_FLIGHT = 5


def per_device(n, queries, kernel, train_feats):
    to_place, to_owner, order = snake(n)
    ahead = [(order[i], order[(i + 1) % n]) for i in range(n)]
    back = [(b, a) for a, b in ahead]
    swap = [(0, 1), (1, 0)]
    row = lax.axis_index("rows")
    feat = lax.axis_index("feat")
    me = row * 2 + feat
    place = to_place(row)
    before = lambda step: to_owner((place + n - step) % n)
    after = lambda step: to_owner((place + step) % n)
    count = queries.shape[0]
    width = kernel.shape[1]
    half = width // 2
    total = count * n

    def product(block):
        partial = jnp.dot(block, kernel, preferred_element_type=jnp.float32)
        return (lax.dynamic_slice_in_dim(partial, feat * half, half, 1),
                lax.dynamic_slice_in_dim(partial, (1 - feat) * half, half, 1))

    devices = 2 * n
    owned = count // 2
    columns = train_feats.shape[0]
    group = 256 // owned
    groups = devices // group
    span = group * owned
    at_group, at_place = me // group, me % group
    shifts = [groups // 2] + [k for k in range(1, groups) if k != groups // 2] + [0]

    table = [me, row * 2 + 1 - feat]
    for step in range(1, n // 2 + 1):
        for owner in (before(step), after(step))[: 1 if 2 * step == n else 2]:
            table += [owner * 2 + feat, owner * 2 + 1 - feat]
    table = jnp.stack(table + [(at_group + shift) % groups for shift in shifts] + [at_place]).astype(jnp.int32)

    blocks = [(row, queries)]
    forward = backward = queries
    for step in range(1, n // 2):
        forward = lax.ppermute(forward, "rows", ahead)
        backward = lax.ppermute(backward, "rows", back)
        blocks += [(before(step), forward), (after(step), backward)]
        if step == 1:
            forward, table = lax.optimization_barrier((forward, table))
    top = lax.ppermute(forward[: count // 2], "rows", ahead)
    bottom = lax.ppermute(backward[count // 2 :], "rows", back)
    keep = jnp.zeros((total, half), jnp.float32)
    give = jnp.zeros((total, half), jnp.float32)
    for owner, block in blocks[:-2]:
        a, b = product(block)
        keep = lax.dynamic_update_slice(keep, a, (owner * count, 0))
        give = lax.dynamic_update_slice(give, b, (owner * count, 0))
    mine = (keep + lax.ppermute(give, "feat", swap)).astype(jnp.bfloat16)
    top, bottom, mine = lax.optimization_barrier((top, bottom, mine))
    late = [product(block) for _, block in blocks[-2:]] + [product(jnp.concatenate([top, bottom]))]
    here = jnp.concatenate([a for a, _ in late])
    there = lax.ppermute(jnp.concatenate([b for _, b in late]), "feat", swap)
    late = (here + there).astype(jnp.bfloat16)
    for k, owner in enumerate([owner for owner, _ in blocks[-2:]] + [before(n // 2)]):
        mine = lax.dynamic_update_slice(mine, late[k * count : (k + 1) * count], (owner * count, 0))

    near = [mine, lax.ppermute(mine, "feat", swap)]
    forward = backward = mine
    for step in range(1, n // 2):
        forward = lax.ppermute(forward, "rows", ahead)
        backward = lax.ppermute(backward, "rows", back)
        if step == n // 2 - 1:
            early = len(near)
            partial = group_part(near, table, 0, devices, train_feats, span, owned)
            forward, backward, squares = lax.optimization_barrier((forward, backward, partial[1]))
            partial = (partial[0], squares)
        for block in (forward, backward):
            near += [block, lax.ppermute(block, "feat", swap)]
    top = lax.ppermute(forward[: total // 2], "rows", ahead)
    bottom = lax.ppermute(backward[total // 2 :], "rows", back)
    partial = group_part(near[early:], table, early, devices, train_feats, span, owned, partial)
    top, bottom, squares = lax.optimization_barrier((top, bottom, partial[1]))
    partial = (partial[0], squares)
    far = [top, lax.ppermute(top, "feat", swap), bottom, lax.ppermute(bottom, "feat", swap)]

    first = group_part(far, table, len(near), devices, train_feats, span, owned, partial, last=True)
    second = group_scores(near, far, table, 1, 1, train_feats, span)
    rest = group_scores(near, far, table, 2, groups - 2, train_feats, span)
    scores = jnp.zeros((owned, devices * columns), jnp.bfloat16)
    order = [(0, turn) for turn in range(group)]
    for turn in range(group):
        order += [(number, turn) for number in (groups - 1, *range(1, groups - 1))]
    going, sources = [], []
    for number, turn in order:
        shift = shifts[number]
        if number == 0:
            block = first[turn]
        else:
            tiles, offset = (second, 0) if number == 1 else (rest, (number - 2) * span)
            block = lax.dynamic_slice_in_dim(tiles, offset + (at_place + turn) % group * owned, owned, 0)
        source = (at_group + groups - shift) % groups * group + (at_place + group - turn) % group
        if shift or turn:
            pairs = [(i, (i // group + shift) % groups * group + (i + turn) % group) for i in range(devices)]
            if len(going) >= IN_FLIGHT:
                block, going[-IN_FLIGHT], behind = lax.optimization_barrier((block, going[-IN_FLIGHT], behind))
            behind = block
            going.append(lax.ppermute(block, ("rows", "feat"), pairs))
            sources.append(source)
        else:
            own = (block, source)
    for block, source in [own] + list(zip(going, sources)):
        scores = lax.dynamic_update_slice(scores, block, (0, source * columns))
    return scores


def solution(mesh):
    placed = (P("rows", "feat"), P(("corpus", "feat"), "rows"), P(("corpus", "rows", "feat"), None))
    return jax.shard_map(
        functools.partial(per_device, mesh.shape["rows"]),
        mesh=mesh,
        in_specs=placed,
        out_specs=P(("rows", "feat"), "corpus"),
        check_vma=False,
    )
```

```python
import functools

import jax
import jax.numpy as jnp
from jax import lax
from jax.experimental import pallas as pl
from jax.experimental.pallas import tpu as pltpu
from jax.sharding import PartitionSpec as P

epsilon = 1e-06


def snake(n):
    if n == 8:
        return (lambda r: jnp.where(r % 2 == 0, r // 2, n - 1 - r // 2),
                lambda p: jnp.where(p < n // 2, 2 * p, 2 * (n - 1 - p) + 1),
                [0, 2, 4, 6, 7, 5, 3, 1])
    return (lambda r: r), (lambda p: p), list(range(n))


def tile_rows(owners, skip, shifts, span, where, *refs):
    n_near = 2 * (owners - 1)
    near, (top, top_other, bottom, bottom_other, train) = refs[:n_near], refs[n_near : n_near + 5]
    scores, left, held, lengths, piece_sems, train_sems = refs[n_near + 5 :]
    width = top.shape[1]
    upper = top.shape[0]
    tile = held.shape[1]
    steps = train.shape[0] // tile

    def stream(j):
        return pltpu.make_async_copy(train.at[pl.ds(pl.multiple_of(j * tile, tile), tile), :], held.at[j % 2], train_sems.at[j % 2])

    def lay(source, first, number, k):
        columns = pl.ds(pl.multiple_of(where[k] * width, width), width)
        return pltpu.make_async_copy(
            source.at[pl.ds(pl.multiple_of(first, span), span), :],
            left.at[pl.ds(number * span, span), columns],
            piece_sems.at[number, k],
        )

    stream(0).start()
    for number in range(len(shifts)):
        first = where[2 * owners + skip + number] * span
        for k, piece in enumerate(near):
            lay(piece, first, number, k).start()

        @pl.when(first < upper)
        def _():
            lay(top, first, number, n_near).start()
            lay(top_other, first, number, n_near + 1).start()

        @pl.when(first >= upper)
        def _():
            lay(bottom, first - upper, number, n_near).start()
            lay(bottom_other, first - upper, number, n_near + 1).start()

    for number in range(len(shifts)):
        for k in range(2 * owners):
            lay(top, 0, number, k).wait()

    sums = 0.0
    for at in range(0, left.shape[1], 128):
        wide = left[:, at : at + 128].astype(jnp.float32)
        sums = sums + wide * wide
    lengths[...] = jnp.broadcast_to(jnp.sqrt(jnp.sum(sums, axis=1, keepdims=True) + epsilon), lengths.shape)

    def step(j, carry):
        @pl.when(j + 1 < steps)
        def _():
            stream(j + 1).start()

        stream(j).wait()
        across = (((1,), (1,)), ((), ()))
        if left.shape[0] < tile:
            raw = lax.dot_general(held[j % 2], left[...], across, preferred_element_type=jnp.float32).T
        else:
            raw = lax.dot_general(left[...], held[j % 2], across, preferred_element_type=jnp.float32)
        for at in range(0, tile, 128):
            columns = pl.ds(pl.multiple_of(j * tile + at, 128), 128)
            scores[:, columns] = (raw[:, at : at + 128] / lengths[...]).astype(scores.dtype)
        return carry

    lax.fori_loop(0, steps, step, 0)


def some_columns(count, base, group_at, last, more, owned, where, *refs):
    near, refs = refs[: 4 if last else count], refs[4 if last else count :]
    train, refs = refs[0], refs[1:]
    if more:
        raw_in, squares_in, refs = refs[0], refs[1], refs[2:]
    if last:
        outs = refs[: len(refs) - (7 if more else 5)]
        refs = refs[len(outs) :]
    else:
        raw_out, squares_out, refs = refs[0], refs[1], refs[2:]
    left, held, piece_sems, train_sems = refs[:4]
    if more:
        before, in_sems = refs[4:6]
    span = left.shape[0]
    group = span // owned
    width = near[0].shape[1]
    tile = held.shape[1]
    steps = train.shape[0] // tile
    first = where[group_at] * span
    place = where[where.shape[0] - 1]

    def stream(j, pair):
        columns = pl.ds(pl.multiple_of(where[base + 2 * pair] // 2 * (2 * width), 2 * width), 2 * width)
        return pltpu.make_async_copy(
            train.at[pl.ds(pl.multiple_of(j * tile, tile), tile), columns],
            held.at[j, :, pl.ds(pair * 2 * width, 2 * width)],
            train_sems.at[j, pair],
        )

    def earlier(j):
        columns = pl.ds(pl.multiple_of(j * tile, tile), tile)
        return pltpu.make_async_copy(raw_in.at[:, columns], before.at[:, columns], in_sems.at[j])

    def lay(source, start, k, turn):
        at = start + lax.rem(place + turn, group) * owned
        return pltpu.make_async_copy(
            source.at[pl.ds(pl.multiple_of(at, owned), owned), :],
            left.at[pl.ds(turn * owned, owned), pl.ds(pl.multiple_of(k // 2 * (2 * width) + where[base + k] % 2 * width, width), width)],
            piece_sems.at[k, turn],
        )

    def lay_all(some, start):
        for k, piece in enumerate(some):
            for turn in range(group):
                lay(piece, start, k, turn).start()

    for pair in range(count // 2):
        stream(0, pair).start()
    if last:
        upper = near[0].shape[0]
        pl.when(first < upper)(lambda: lay_all(near[:2], first))
        pl.when(first >= upper)(lambda: lay_all(near[2:], first - upper))
    else:
        lay_all(near, first)
    for j in range(1, steps):
        for pair in range(count // 2):
            stream(j, pair).start()
    if more:
        for j in range(steps):
            earlier(j).start()
    for k in range(count):
        for turn in range(group):
            lay(near[0], 0, k, turn).wait()

    squared = squares_in[...] if more else 0.0
    for at in range(0, left.shape[1], 128):
        wide = left[:, at : at + 128].astype(jnp.float32)
        squared = squared + wide * wide
    if last:
        lengths = refs[-1]
        lengths[...] = jnp.broadcast_to(jnp.sqrt(jnp.sum(squared, axis=1, keepdims=True) + epsilon), lengths.shape)
    else:
        squares_out[...] = squared

    def step(j, carry):
        for pair in range(count // 2):
            stream(j, pair).wait()
        across = (((1,), (1,)), ((), ()))
        raw = lax.dot_general(left[...], held[j], across, preferred_element_type=jnp.float32)
        columns = pl.ds(pl.multiple_of(j * tile, tile), tile)
        if more:
            earlier(j).wait()
            raw = before[:, columns] + raw
        if not last:
            raw_out[:, columns] = raw
            return carry
        for at in range(0, tile, 128):
            part = (raw[:, at : at + 128] / lengths[...]).astype(outs[0].dtype)
            for turn in range(group):
                outs[turn][:, pl.ds(pl.multiple_of(j * tile + at, 128), 128)] = part[turn * owned : (turn + 1) * owned]
        return carry

    lax.fori_loop(0, steps, step, 0)


def group_part(pieces, table, base, group_at, train_feats, span, owned, earlier=(), last=False):
    columns = train_feats.shape[0]
    count = len(pieces) // 2 if last else len(pieces)
    depth = count * pieces[0].shape[1]
    tile = 1024
    group = span // owned
    anywhere, inside = pl.BlockSpec(memory_space=pl.ANY), pl.BlockSpec(memory_space=pltpu.VMEM)
    in_specs = [pl.BlockSpec(memory_space=pltpu.SMEM)] + [anywhere] * (len(pieces) + 1)
    scratch = [
        pltpu.VMEM((span, depth), jnp.bfloat16),
        pltpu.VMEM((columns // tile, tile, depth), jnp.bfloat16),
        pltpu.SemaphoreType.DMA((count, group)),
        pltpu.SemaphoreType.DMA((columns // tile, count // 2)),
    ]
    if earlier:
        in_specs += [anywhere, inside]
        scratch += [pltpu.VMEM((span, columns), jnp.float32), pltpu.SemaphoreType.DMA((columns // tile,))]
    if last:
        scratch += [pltpu.VMEM((span, 128), jnp.float32)]
        out_shape = (jax.ShapeDtypeStruct((owned, columns), jnp.bfloat16),) * group
        out_specs = (inside,) * group
    else:
        out_shape = (jax.ShapeDtypeStruct((span, columns), jnp.float32), jax.ShapeDtypeStruct((span, 128), jnp.float32))
        out_specs = (inside, inside)
    return pl.pallas_call(
        functools.partial(some_columns, count, base, group_at, last, bool(earlier), owned),
        out_shape=out_shape,
        in_specs=in_specs,
        out_specs=out_specs,
        scratch_shapes=scratch,
        compiler_params=pltpu.CompilerParams(vmem_limit_bytes=VMEM_LIMIT),
        cost_estimate=pl.CostEstimate(flops=2 * span * columns * depth, bytes_accessed=2 * columns * depth, transcendentals=0),
    )(table, *pieces, train_feats, *earlier)


def group_scores(near, far, where, skip, targets, train_feats, span):
    owners = len(near) // 2 + 1
    columns, depth = train_feats.shape
    rows = span * targets
    tile = 512
    anywhere = pl.BlockSpec(memory_space=pl.ANY)
    return pl.pallas_call(
        functools.partial(tile_rows, owners, skip, tuple(range(targets)), span),
        out_shape=jax.ShapeDtypeStruct((rows, columns), jnp.bfloat16),
        in_specs=[pl.BlockSpec(memory_space=pltpu.SMEM)] + [anywhere] * (len(near) + len(far) + 1),
        out_specs=pl.BlockSpec(memory_space=pltpu.VMEM),
        scratch_shapes=[
            pltpu.VMEM((rows, depth), jnp.bfloat16),
            pltpu.VMEM((2, tile, depth), jnp.bfloat16),
            pltpu.VMEM((rows, 128), jnp.float32),
            pltpu.SemaphoreType.DMA((targets, 2 * owners)),
            pltpu.SemaphoreType.DMA((2,)),
        ],
        compiler_params=pltpu.CompilerParams(vmem_limit_bytes=VMEM_LIMIT),
        cost_estimate=pl.CostEstimate(flops=2 * rows * columns * depth, bytes_accessed=2 * columns * depth, transcendentals=0),
    )(where, *near, *far, train_feats)


VMEM_LIMIT = 58 * 2**20
IN_FLIGHT = 5


def per_device(n, queries, kernel, train_feats):
    to_place, to_owner, order = snake(n)
    ahead = [(order[i], order[(i + 1) % n]) for i in range(n)]
    back = [(b, a) for a, b in ahead]
    swap = [(0, 1), (1, 0)]
    row = lax.axis_index("rows")
    feat = lax.axis_index("feat")
    me = row * 2 + feat
    place = to_place(row)
    before = lambda step: to_owner((place + n - step) % n)
    after = lambda step: to_owner((place + step) % n)
    count = queries.shape[0]
    width = kernel.shape[1]
    half = width // 2
    total = count * n

    def product(block):
        partial = jnp.dot(block, kernel, preferred_element_type=jnp.float32)
        return (lax.dynamic_slice_in_dim(partial, feat * half, half, 1),
                lax.dynamic_slice_in_dim(partial, (1 - feat) * half, half, 1))

    devices = 2 * n
    owned = count // 2
    columns = train_feats.shape[0]
    group = 256 // owned
    groups = devices // group
    span = group * owned
    at_group, at_place = me // group, me % group
    shifts = [groups // 2] + [k for k in range(1, groups) if k != groups // 2] + [0]

    table = [me, row * 2 + 1 - feat]
    for step in range(1, n // 2 + 1):
        for owner in (before(step), after(step))[: 1 if 2 * step == n else 2]:
            table += [owner * 2 + feat, owner * 2 + 1 - feat]
    table = jnp.stack(table + [(at_group + shift) % groups for shift in shifts] + [at_place]).astype(jnp.int32)

    blocks = [(row, queries)]
    forward = backward = queries
    for step in range(1, n // 2):
        forward = lax.ppermute(forward, "rows", ahead)
        backward = lax.ppermute(backward, "rows", back)
        blocks += [(before(step), forward), (after(step), backward)]
        if step == 1:
            forward, table = lax.optimization_barrier((forward, table))
    top = lax.ppermute(forward[: count // 2], "rows", ahead)
    bottom = lax.ppermute(backward[count // 2 :], "rows", back)
    keep = jnp.zeros((total, half), jnp.float32)
    give = jnp.zeros((total, half), jnp.float32)
    for owner, block in blocks[:-2]:
        a, b = product(block)
        keep = lax.dynamic_update_slice(keep, a, (owner * count, 0))
        give = lax.dynamic_update_slice(give, b, (owner * count, 0))
    mine = (keep + lax.ppermute(give, "feat", swap)).astype(jnp.bfloat16)
    top, bottom, mine = lax.optimization_barrier((top, bottom, mine))
    late = [product(block) for _, block in blocks[-2:]] + [product(jnp.concatenate([top, bottom]))]
    here = jnp.concatenate([a for a, _ in late])
    there = lax.ppermute(jnp.concatenate([b for _, b in late]), "feat", swap)
    late = (here + there).astype(jnp.bfloat16)
    for k, owner in enumerate([owner for owner, _ in blocks[-2:]] + [before(n // 2)]):
        mine = lax.dynamic_update_slice(mine, late[k * count : (k + 1) * count], (owner * count, 0))

    near = [mine, lax.ppermute(mine, "feat", swap)]
    forward = backward = mine
    for step in range(1, n // 2):
        forward = lax.ppermute(forward, "rows", ahead)
        backward = lax.ppermute(backward, "rows", back)
        if step == n // 2 - 1:
            early = len(near)
            partial = group_part(near, table, 0, devices, train_feats, span, owned)
            forward, backward, squares = lax.optimization_barrier((forward, backward, partial[1]))
            partial = (partial[0], squares)
        for block in (forward, backward):
            near += [block, lax.ppermute(block, "feat", swap)]
    top = lax.ppermute(forward[: total // 2], "rows", ahead)
    bottom = lax.ppermute(backward[total // 2 :], "rows", back)
    partial = group_part(near[early:], table, early, devices, train_feats, span, owned, partial)
    top, bottom, squares = lax.optimization_barrier((top, bottom, partial[1]))
    partial = (partial[0], squares)
    far = [top, lax.ppermute(top, "feat", swap), bottom, lax.ppermute(bottom, "feat", swap)]

    first = group_part(far, table, len(near), devices, train_feats, span, owned, partial, last=True)
    second = group_scores(near, far, table, 1, 1, train_feats, span)
    rest = group_scores(near, far, table, 2, groups - 2, train_feats, span)
    scores = jnp.zeros((owned, devices * columns), jnp.bfloat16)
    order = [(0, turn) for turn in range(group)]
    for turn in range(group):
        order += [(number, turn) for number in (groups - 1, *range(1, groups - 1))]
    going, sources = [], []
    for number, turn in order:
        shift = shifts[number]
        if number == 0:
            block = first[turn]
        else:
            tiles, offset = (second, 0) if number == 1 else (rest, (number - 2) * span)
            block = lax.dynamic_slice_in_dim(tiles, offset + (at_place + turn) % group * owned, owned, 0)
        source = (at_group + groups - shift) % groups * group + (at_place + group - turn) % group
        if shift or turn:
            pairs = [(i, (i // group + shift) % groups * group + (i + turn) % group) for i in range(devices)]
            if len(going) >= IN_FLIGHT:
                block, going[-IN_FLIGHT], behind = lax.optimization_barrier((block, going[-IN_FLIGHT], behind))
            behind = block
            going.append(lax.ppermute(block, ("rows", "feat"), pairs))
            sources.append(source)
        else:
            own = (block, source)
    for block, source in [own] + list(zip(going, sources)):
        scores = lax.dynamic_update_slice(scores, block, (0, source * columns))
    return scores


def solution(mesh):
    placed = (P("rows", "feat"), P(("corpus", "feat"), "rows"), P(("corpus", "rows", "feat"), None))
    return jax.shard_map(
        functools.partial(per_device, mesh.shape["rows"]),
        mesh=mesh,
        in_specs=placed,
        out_specs=P(("rows", "feat"), "corpus"),
        check_vma=False,
    )
```
